256 devices in a mesh: band: 8 (over y, core), space: 32 (over x, z).
Axes of the slice: x: 4, y: 4, z: 8, core: 2. Of those that a mesh axis runs over, the one named last changes fastest.
Arguments:
- left_factor: bfloat16 [8, 32768, 2048], P('band', 'space'), may hold values from -0.1875 to 0.1875
- right_factor: bfloat16 [8, 2048, 32768], P('band', None, 'space'), may hold values from -0.125 to 0.125
- data: bfloat16 [8, 256, 32768], P('band', None, 'space'), may hold values from -6 to 6
Outputs:
- solution: float32 [256, 32768], P('band', 'space')
- residual: float32 [256, 32768], P('band', 'space')
The draws below stay inside these ranges and needn't reach their ends.
All inputs are finite; a program needn't handle non-finite values.
Results may differ from the reference program's by a relative error of at most 0.03.
Values may be sent and summed in bfloat16 or wider, within the bound.
No kernel may reach another device: no remote copies, remote signals or barrier semaphores. Data moves between devices by JAX's collectives and lax.ppermute only.
A program may use at most 64 MiB of HBM per device.

```python
import math
import jax
import jax.numpy as jnp

RANK = 64
CELLS = 1024
IMAGES = 256
ITERS = 2
BANDS = 8
GRID = 32768
N_SPACE = 32


def draw_data(key, part):
    key = jax.random.fold_in(key, 7)
    key_base, key_rows = jax.random.split(key, 2)
    shape = (BANDS, IMAGES, GRID)
    base = jnp.clip(jax.random.normal(key_base, shape, jnp.float32), -4.0, 4.0)
    rows = jnp.exp(jax.random.uniform(key_rows, (1, IMAGES, 1), jnp.float32) * math.log(10.0))
    blocks = GRID // CELLS
    which = (jnp.arange(GRID, dtype=jnp.int32) // CELLS).astype(jnp.float32)
    rising = 1.0 + 2.0 * which / max(blocks - 1, 1)
    return (0.05 * base * rows * rising[None, None, :]).astype(jnp.bfloat16)


def shard_levels(rng, dims, cuts, least, high):
    factor_of, own = 1.0, jax.random.fold_in(rng, 6)
    for position, blocks in cuts:
        steps = jnp.exp(jax.random.uniform(jax.random.fold_in(own, position), (blocks,), jnp.float32, least / len(cuts), high / len(cuts)))
        factor_of = factor_of * jnp.repeat(steps, dims[position] // blocks).reshape([-1 if axis == position else 1 for axis in range(len(dims))])
    return factor_of


def gaussian(key, extent, deviation, reach, cuts=(), kind=jnp.bfloat16):
    drawn = jax.random.normal(key, extent, jnp.float32) * deviation
    if len(cuts) > 0:
        drawn = shard_levels(key, extent, cuts, -0.22, 0.18) * drawn
    return jnp.clip(drawn, min=-reach, max=reach).astype(kind)


def setup_inputs(seed: int = 0) -> dict:
    splits = jax.random.split(jax.random.key(seed), 4)
    return {
        "left_factor": gaussian(splits[0], (BANDS, GRID, N_SPACE * RANK), CELLS ** -0.5, 0.1875, ((0, 8), (1, 32))),
        "right_factor": gaussian(splits[1], (BANDS, N_SPACE * RANK, GRID), (N_SPACE * RANK) ** -0.5, 0.125, ((0, 8), (2, 32))),
        "data": draw_data(jax.random.fold_in(splits[3], 71), 0),
    }


damping = 1.0


def forward(image_bf, left_band, right_band):
    blocks = N_SPACE
    left_full = left_band.astype(jnp.float32).reshape(blocks, CELLS, blocks * RANK)
    pieces = image_bf.astype(jnp.float32).reshape(IMAGES, blocks, CELLS)
    coeff = jnp.einsum('vsi,sij->svj', pieces, left_full).astype(jnp.bfloat16)
    coeff = coeff.reshape(blocks, IMAGES, blocks, RANK).transpose(2, 1, 0, 3).reshape(blocks, IMAGES, blocks * RANK)
    right_full = right_band.astype(jnp.float32).reshape(blocks * RANK, blocks, CELLS)
    result = jnp.einsum('tvj,jtc->vtc', coeff.astype(jnp.float32), right_full)
    return result.reshape(IMAGES, blocks * CELLS)


def adjoint(data_bf, left_band, right_band):
    blocks = N_SPACE
    right_full = right_band.astype(jnp.float32).reshape(blocks * RANK, blocks, CELLS)
    pieces = data_bf.astype(jnp.float32).reshape(IMAGES, blocks, CELLS)
    back = jnp.einsum('vtc,jtc->tvj', pieces, right_full).astype(jnp.bfloat16)
    back = back.reshape(blocks, IMAGES, blocks, RANK).transpose(2, 1, 0, 3).reshape(blocks, IMAGES, blocks * RANK)
    left_full = left_band.astype(jnp.float32).reshape(blocks, CELLS, blocks * RANK)
    result = jnp.einsum('svj,sij->vsi', back.astype(jnp.float32), left_full)
    return result.reshape(IMAGES, blocks * CELLS)


def normal(direction, left_factor, right_factor):
    rounded = direction.astype(jnp.bfloat16)
    total = damping * direction
    for band_index in range(BANDS):
        seen = forward(rounded, left_factor[band_index], right_factor[band_index]).astype(jnp.bfloat16)
        total = total + adjoint(seen, left_factor[band_index], right_factor[band_index])
    return total


def reference(left_factor, right_factor, data):
    residual = jnp.zeros((IMAGES, GRID), jnp.float32)
    for band_index in range(BANDS):
        residual = residual + adjoint(data[band_index], left_factor[band_index], right_factor[band_index])
    solution = jnp.zeros((IMAGES, GRID), jnp.float32)
    direction = residual
    norm_now = jnp.sum(residual * residual, axis=1)
    for step in range(ITERS):
        image = normal(direction, left_factor, right_factor)
        curv = jnp.sum(direction * image, axis=1)
        alpha = norm_now / curv
        solution = solution + alpha[:, None] * direction
        residual = residual - alpha[:, None] * image
        norm_next = jnp.sum(residual * residual, axis=1)
        direction = residual + (norm_next / norm_now)[:, None] * direction
        norm_now = norm_next
    return solution, residual
```

```python
import jax
import jax.numpy as jnp
from jax import lax
from jax.sharding import Mesh, PartitionSpec as P

NCH = 1
damping = 1.0
BAND = "band"
SPACE = "space"
f32, bf16 = jnp.float32, jnp.bfloat16


def split(value):
    high = value.astype(bf16)
    return high, (value - high.astype(f32)).astype(bf16)


def per_device(left_factor, right_factor, data):
    left, right = left_factor[0], right_factor[0]
    images = data.shape[1]
    cells, width = left.shape
    bands, blocks = lax.axis_size(BAND), lax.axis_size(SPACE)
    rank = width // blocks
    extra = 8
    m = images // NCH
    share = m // bands
    leftT, rightT = left.T, right.T
    leftT, rightT = lax.optimization_barrier((leftT, rightT))

    def exchange(v):
        return lax.all_to_all(v, SPACE, 0, 0, tiled=True)

    def send(back, scalars=None):
        back = back.reshape(blocks, rank, m)
        if scalars is None:
            return exchange(back), None
        rows = []
        for s in scalars:
            rows += list(split(s))
        rows = jnp.stack(rows + [jnp.zeros_like(rows[0])] * (extra - len(rows)))
        got = exchange(jnp.concatenate([back, jnp.broadcast_to(rows[None], (blocks, extra, m))], axis=1))
        sums = got[:, rank:, :].astype(f32).sum(0)
        return got[:, :rank, :], [sums[2 * i] + sums[2 * i + 1] for i in range(len(scalars))]

    def reduce_band(recv, scalars=None):
        part = lax.dot_general(left, recv.reshape(width, m), (((1,), (0,)), ((), ())), preferred_element_type=f32)
        part = part.T.astype(bf16)
        if scalars is not None:
            cols = []
            for s in scalars:
                cols += list(split(s))
            cols = jnp.stack(cols, axis=1)
            cols = jnp.pad(cols, ((0, 0), (0, 128 - cols.shape[1])))
            part = jnp.concatenate([part, cols], axis=1)
        got = lax.all_to_all(part.reshape(bands, share, part.shape[1]), BAND, 0, 0, tiled=True)
        got = got.astype(f32).sum(0)
        if scalars is None:
            return got, None
        tail = got[:, cells:]
        return got[:, :cells], [(tail[:, 2 * i] + tail[:, 2 * i + 1])[:, None] for i in range(len(scalars))]

    def gather(v):
        v = jnp.broadcast_to(v.astype(bf16)[None], (bands,) + v.shape)
        return lax.all_to_all(v, BAND, 0, 0, tiled=True).reshape(m, cells)

    def back_of(w, dims):
        return lax.dot_general(right, w, (((1,), (dims,)), ((), ())), preferred_element_type=f32).astype(bf16)

    def forward(p):
        coeff = lax.dot_general(leftT, p, (((1,), (1,)), ((), ())), preferred_element_type=f32).astype(bf16)
        recv = exchange(coeff.reshape(blocks, rank, m)).reshape(width, m)
        return lax.dot_general(rightT, recv, (((1,), (0,)), ((), ())), preferred_element_type=f32)

    def sumsq(a, b, axis):
        return jnp.sum(a.astype(f32) * b.astype(f32), axis=axis)

    sols, ress = [], []
    st = [dict() for _ in range(NCH)]
    for c in range(NCH):
        d = data[0, c * m:(c + 1) * m]
        recv, _ = send(back_of(d, 1))
        r0, _ = reduce_band(recv)
        p0 = gather(r0)
        s0 = forward(p0)
        pp = sumsq(p0, p0, 1) / bands
        cc = sumsq(s0, s0, 0) + damping * pp
        recv, sc = send(back_of(s0.astype(bf16), 0), [pp, cc])
        q0, (rr0, c0) = reduce_band(recv, sc)
        q0 = q0 + damping * r0
        a0 = rr0 / c0
        r1 = r0 - a0 * q0
        p1 = gather(r1)
        s1 = forward(p1)
        rp = sumsq(p1, p1, 1) / bands
        rx = sumsq(p1, p0, 1) / bands
        ss = sumsq(s1, s1, 0) + damping * rp
        sx = sumsq(s1, s0, 0) + damping * rx
        recv, sc = send(back_of(s1.astype(bf16), 0), [rp, ss, sx])
        q1, (rr1, n11, n01) = reduce_band(recv, sc)
        q1 = q1 + damping * r1
        b0 = rr1 / rr0
        c1 = n11 + 2 * b0 * n01 + b0 * b0 * c0
        a1 = rr1 / c1
        sols.append(a0 * r0 + a1 * (r1 + b0 * r0))
        ress.append(r1 - a1 * (q1 + b0 * q0))
    if NCH == 1:
        return sols[0], ress[0]
    return jnp.concatenate(sols), jnp.concatenate(ress)


def solution(mesh):
    return jax.shard_map(
        per_device,
        mesh=mesh,
        in_specs=(P("band", "space", None), P("band", None, "space"), P("band", None, "space")),
        out_specs=(P("band", "space"), P("band", "space")),
        check_vma=False,
    )
```

```python
import functools
import jax
import jax.numpy as jnp
from jax import lax
from jax.experimental import pallas as pl
from jax.experimental.pallas import tpu as pltpu
from jax.sharding import PartitionSpec as P

damping = 1.0
BAND = "band"
SPACE = "space"
f32, bf16 = jnp.float32, jnp.bfloat16
EXTRA = 8
TAIL = 128
STEP = 256

VMEM = pl.BlockSpec(memory_space=pltpu.VMEM)
SMEM = pl.BlockSpec(memory_space=pltpu.SMEM)


def order_of(blocks):
    if blocks != 32:
        return list(range(blocks))
    return [x * 8 + high * 4 + low for low in range(4) for x in range(4) for high in range(2)]


def dot(a, b, dims=((1,), (0,))):
    return lax.dot_general(a, b, (dims, ((), ())), preferred_element_type=f32)


def call(body, outs, scratch, flops, args, specs=None):
    moved = sum(a.size * a.dtype.itemsize for a in args) + sum(o.size * o.dtype.itemsize for o in outs)
    return pl.pallas_call(
        body,
        out_shape=outs,
        in_specs=specs or [VMEM] * len(args),
        out_specs=[VMEM] * len(outs),
        scratch_shapes=scratch,
        cost_estimate=pl.CostEstimate(flops=flops, bytes_accessed=moved, transcendentals=0),
        compiler_params=pltpu.CompilerParams(vmem_limit_bytes=40 * 1024 * 1024),
    )(*args)


def shape(dims, kind):
    return jax.ShapeDtypeStruct(dims, kind)


def put_blocks(out, rows, first, place, rank):
    for i in range(rows.shape[0] // rank):
        out[place[first + i], :rank, :] = rows[i * rank:(i + 1) * rank]


def take_blocks(got, natural, order, rank):
    for q, s in enumerate(order):
        natural[s * rank:(s + 1) * rank, :] = got[q, :rank, :]


def first_body(place, rank, share, perm, d, r, out, dp):
    for k in range(d.shape[0] // share):
        dp[k * share:(k + 1) * share, :] = d[pl.ds(pl.multiple_of(perm[k] * share, share), share), :]
    step = min(STEP, r.shape[0])
    for j in range(0, r.shape[0], step):
        put_blocks(out, dot(r[j:j + step, :], dp[...], ((1,), (1,))).astype(bf16), j // rank, place, rank)


def adjoint_body(order, rank, tail, got, l, own, oth, natural):
    take_blocks(got, natural, order, rank)
    cells, half = l.shape[0], own.shape[0]
    step = min(STEP, cells)
    for j in range(0, cells, step):
        t = dot(l[j:j + step, :], natural[...]).T
        own[:, j:j + step] = t[:half]
        oth[:, j:j + step] = t[half:].astype(bf16)
    if tail:
        rows = got[0, rank:, :].astype(f32)
        for q in range(1, len(order)):
            rows = rows + got[q, rank:, :].astype(f32)
        rows = rows[:4] + rows[4:]
        high = rows.astype(bf16).astype(f32)
        t = jnp.concatenate([high, rows - high, jnp.zeros((TAIL - 8, rows.shape[1]), f32)], axis=0).T
        own[:, cells:] = t[:half]
        oth[:, cells:] = t[half:].astype(bf16)


def pair_body(cells, tail, own, got, mine, *rest):
    share = mine.shape[0]
    total = own[:, :cells] + got[:, :cells].astype(f32)
    mine[:, :cells] = total[:share]
    for k, out in enumerate(rest):
        out[:, :cells] = total[(k + 1) * share:(k + 2) * share].astype(bf16)
    if tail:
        part = own[:, cells:] + got[:, cells:].astype(f32)
        lane = lax.broadcasted_iota(jnp.int32, part.shape, 1)
        both = part + pltpu.roll(part, TAIL - 4, 1)
        high = both.astype(bf16).astype(f32)
        low = pltpu.roll(both - high, 4, 1)
        part = jnp.where(lane < 4, high, jnp.where(lane < 8, low, 0.0))
        mine[:, cells:] = part[:share]
        for k, out in enumerate(rest):
            out[:, cells:] = part[(k + 1) * share:(k + 2) * share].astype(bf16)


def coeff_body(place, rank, bands, cross, pa, pb, *rest):
    if cross:
        qa, qb, l, out, norms, p = rest
    else:
        l, out, norms, p = rest
    half = pa.shape[0]
    p[:half, :] = pa[...]
    p[half:, :] = pb[...]
    width = l.shape[1]
    step = min(STEP, width)
    for j in range(0, width, step):
        put_blocks(out, dot(p[...], l[:, j:j + step]).astype(bf16).T, j // rank, place, rank)
    lane = lax.broadcasted_iota(jnp.int32, (half, TAIL), 1)
    for h, (now, old) in enumerate(((pa, qa), (pb, qb)) if cross else ((pa, None), (pb, None))):
        v = now[...].astype(f32)
        col = jnp.where(lane == 0, jnp.sum(v * v, axis=1, keepdims=True) * (1.0 / bands), 0.0)
        if cross:
            col = jnp.where(lane == 1, jnp.sum(v * old[...].astype(f32), axis=1, keepdims=True) * (1.0 / bands), col)
        norms[h * half:(h + 1) * half, :] = col


def middle_body(order, place, rank, cross, got, norms, r, *rest):
    if cross:
        old, out, seen, natural, turned = rest
    else:
        out, seen, natural, turned = rest
    take_blocks(got, natural, order, rank)
    width, cells = r.shape
    step = min(STEP, width)
    for j in range(0, width, step):
        turned[:, j:j + step] = natural[j:j + step, :].T
    step = min(STEP, cells)
    square = product = None
    for j in range(0, cells, step):
        s = dot(turned[...], r[:, j:j + step])
        seen[:, j:j + step] = s.astype(bf16)
        a = jnp.sum(s * s, axis=1, keepdims=True)
        square = a if square is None else square + a
        if cross:
            a = jnp.sum(s * old[:, j:j + step].astype(f32), axis=1, keepdims=True)
            product = a if product is None else product + a
    step = min(STEP, width)
    for j in range(0, width, step):
        back = dot(r[j:j + step, :], seen[...], ((1,), (1,))).astype(bf16)
        put_blocks(out, back, j // rank, place, rank)
    tile = norms[...]
    lane = lax.broadcasted_iota(jnp.int32, tile.shape, 1)
    pp, px = tile[:, 0:1], tile[:, 1:2]
    cols = jnp.where(lane == 0, pp, jnp.where(lane == 1, square + damping * pp, 0.0))
    if cross:
        cols = jnp.where(lane == 2, product + damping * px, cols)
    rows = cols.T[:4]
    high = rows.astype(bf16).astype(f32)
    rows = jnp.concatenate([high, rows - high], axis=0).astype(bf16)
    for q in range(len(order)):
        out[q, rank:, :] = rows


def per_device(left_factor, right_factor, data):
    left, right, d = left_factor[0], right_factor[0], data[0]
    m, cells = d.shape
    width = left.shape[1]
    bands, blocks = lax.axis_size(BAND), lax.axis_size(SPACE)
    rank = width // blocks
    share, half, pairs = m // bands, m // 2, bands // 2
    order = order_of(blocks)
    place = [order.index(s) for s in range(blocks)]
    me = lax.axis_index(BAND)
    work = 2 * m * cells * width

    def exchange(v):
        return lax.all_to_all(v, SPACE, 0, 0, tiled=True, axis_index_groups=[order])

    def swap(v, flip):
        return lax.ppermute(v, BAND, [(i, i ^ flip) for i in range(bands)])

    def reduce_band(got, tail):
        columns = cells + (TAIL if tail else 0)
        own, oth = call(
            functools.partial(adjoint_body, order, rank, tail),
            [shape((half, columns), f32), shape((half, columns), bf16)],
            [pltpu.VMEM((width, m), bf16)], work, (got, left),
        )
        mine, *rest = call(
            functools.partial(pair_body, cells, tail),
            [shape((share, columns), f32)] + [shape((share, columns), bf16)] * (pairs - 1),
            [], half * columns, (own, swap(oth, 1)),
        )
        total = mine
        for k in range(1, pairs):
            total = total + swap(rest[k - 1], 2 * k).astype(f32)
        if not tail:
            return total, None
        return total[:, :cells], total[:, cells:cells + 4] + total[:, cells + 4:cells + 8]

    def gather(v):
        v = v.astype(bf16)
        v = jnp.concatenate([v] + [swap(v, 2 * k) for k in range(1, pairs)], axis=0)
        return v, swap(v, 1)

    def forward(now, old=()):
        coeff, norms = call(
            functools.partial(coeff_body, place, rank, bands, bool(old)),
            [shape((blocks, rank, m), bf16), shape((m, TAIL), f32)],
            [pltpu.VMEM((m, cells), bf16)], work, (*now, *old, left),
        )
        return exchange(coeff), norms

    def middle(got, norms, old=()):
        out, seen = call(
            functools.partial(middle_body, order, place, rank, bool(old)),
            [shape((blocks, rank + EXTRA, m), bf16), shape((m, cells), bf16)],
            [pltpu.VMEM((width, m), bf16), pltpu.VMEM((m, width), bf16)], 2 * work, (got, norms, right, *old),
        )
        return exchange(out), seen

    perm = jnp.stack([me ^ (2 * y + c) for c in range(2) for y in range(pairs)]).astype(jnp.int32)
    back = call(
        functools.partial(first_body, place, rank, share),
        [shape((blocks, rank, m), bf16)], [pltpu.VMEM((m, cells), bf16)], work, (perm, d, right),
        [SMEM, VMEM, VMEM],
    )[0]
    got = exchange(back)
    r0, _ = reduce_band(got, False)
    p0 = gather(r0)
    got, norms = forward(p0)
    got, s0 = middle(got, norms)
    q0, sums = reduce_band(got, True)
    rr0, c0 = sums[:, 0:1], sums[:, 1:2]
    q0 = q0 + damping * r0
    a0 = rr0 / c0
    r1 = r0 - a0 * q0
    p1 = gather(r1)
    got, norms = forward(p1, p0)
    got, _ = middle(got, norms, (s0,))
    q1, sums = reduce_band(got, True)
    rr1, n11, n01 = sums[:, 0:1], sums[:, 1:2], sums[:, 2:3]
    q1 = q1 + damping * r1
    b0 = rr1 / rr0
    c1 = n11 + 2 * b0 * n01 + b0 * b0 * c0
    a1 = rr1 / c1
    return a0 * r0 + a1 * (r1 + b0 * r0), r1 - a1 * (q1 + b0 * q0)


def solution(mesh):
    return jax.shard_map(
        per_device,
        mesh=mesh,
        in_specs=(P("band", "space", None), P("band", None, "space"), P("band", None, "space")),
        out_specs=(P("band", "space"), P("band", "space")),
        check_vma=False,
    )
```

```python
import functools
import jax
import jax.numpy as jnp
from jax import lax
from jax.experimental import pallas as pl
from jax.experimental.pallas import tpu as pltpu
from jax.sharding import PartitionSpec as P

damping = 1.0
BAND = "band"
SPACE = "space"
f32, bf16 = jnp.float32, jnp.bfloat16
EXTRA = 8
TAIL = 128
STEP = 256

VMEM = pl.BlockSpec(memory_space=pltpu.VMEM)
SMEM = pl.BlockSpec(memory_space=pltpu.SMEM)


def order_of(blocks):
    if blocks != 32:
        return list(range(blocks))
    return [x * 8 + high * 4 + low for low in range(4) for x in range(4) for high in range(2)]


def dot(a, b, dims=((1,), (0,))):
    return lax.dot_general(a, b, (dims, ((), ())), preferred_element_type=f32)


def call(body, outs, scratch, flops, args, specs=None):
    moved = sum(a.size * a.dtype.itemsize for a in args) + sum(o.size * o.dtype.itemsize for o in outs)
    return pl.pallas_call(
        body,
        out_shape=outs,
        in_specs=specs or [VMEM] * len(args),
        out_specs=[VMEM] * len(outs),
        scratch_shapes=scratch,
        cost_estimate=pl.CostEstimate(flops=flops, bytes_accessed=moved, transcendentals=0),
        compiler_params=pltpu.CompilerParams(vmem_limit_bytes=40 * 1024 * 1024),
    )(*args)


def shape(dims, kind):
    return jax.ShapeDtypeStruct(dims, kind)


def put_blocks(out, rows, first, place, rank):
    half = rows.shape[1] // 2
    for i in range(rows.shape[0] // rank):
        block = rows[i * rank:(i + 1) * rank]
        out[place[first + i], :rank, :] = block[:, :half]
        out[place[first + i], rank:2 * rank, :] = block[:, half:]


def take_blocks(got, natural, order, rank):
    half = got.shape[2]
    for q, s in enumerate(order):
        natural[s * rank:(s + 1) * rank, :half] = got[q, :rank, :]
        natural[s * rank:(s + 1) * rank, half:] = got[q, rank:2 * rank, :]


def first_body(place, rank, share, perm, d, r, out, dp):
    for k in range(d.shape[0] // share):
        dp[k * share:(k + 1) * share, :] = d[pl.ds(pl.multiple_of(perm[k] * share, share), share), :]
    step = min(STEP, r.shape[0])
    for j in range(0, r.shape[0], step):
        put_blocks(out, dot(r[j:j + step, :], dp[...], ((1,), (1,))).astype(bf16), j // rank, place, rank)


def adjoint_body(order, rank, scalars, got, l, own, oth, natural):
    take_blocks(got, natural, order, rank)
    cells, half = l.shape[0], own.shape[0]
    step = min(STEP, cells)
    for j in range(0, cells, step):
        t = dot(l[j:j + step, :], natural[...]).T
        own[:, j:j + step] = t[:half]
        oth[:, j:j + step] = t[half:].astype(bf16)
    if scalars:
        rows = got[0, 2 * rank:, :].astype(f32)
        for q in range(1, len(order)):
            rows = rows + got[q, 2 * rank:, :].astype(f32)
        rows = jnp.concatenate([rows[:4], rows[4:]], axis=1)
        first = rows[0:1] + rows[1:2]
        zero = jnp.zeros_like(first)
        if scalars == 2:
            rows = [first, rows[2:3] + rows[3:4], zero, zero]
        else:
            rows = [first, rows[2:3], rows[3:4], zero]
        rows = jnp.concatenate(rows, axis=0)
        high = rows.astype(bf16).astype(f32)
        t = jnp.concatenate([high, rows - high, jnp.zeros((TAIL - 8, rows.shape[1]), f32)], axis=0).T
        own[:, cells:] = t[:half]
        oth[:, cells:] = t[half:].astype(bf16)


def resplit(part):
    lane = lax.broadcasted_iota(jnp.int32, part.shape, 1)
    both = part + pltpu.roll(part, TAIL - 4, 1)
    high = both.astype(bf16).astype(f32)
    return jnp.where(lane < 4, high, jnp.where(lane < 8, pltpu.roll(both - high, 4, 1), 0.0))


def pair_body(cells, tail, own, got, low, high):
    mid = cells // 2
    low[...] = (own[:, :mid] + got[:, :mid].astype(f32)).astype(bf16)
    high[:, :mid] = (own[:, mid:cells] + got[:, mid:cells].astype(f32)).astype(bf16)
    if tail:
        high[:, mid:] = resplit(own[:, cells:] + got[:, cells:].astype(f32)).astype(bf16)


def summed(v, got, k, b, share, columns):
    rows, far = slice(b * share, (b + 1) * share), slice((b ^ k) * share, ((b ^ k) + 1) * share)
    return v[rows, columns].astype(f32) + got[far, columns].astype(f32)


def step_body(k, pairs, cells, v, got, out):
    share = v.shape[0] // pairs
    for b in range(pairs):
        rows = slice(b * share, (b + 1) * share)
        out[rows, :cells] = summed(v, got, k, b, share, slice(0, cells)).astype(bf16)
        if v.shape[1] > cells:
            out[rows, cells:] = resplit(summed(v, got, k, b, share, slice(cells, None))).astype(bf16)


def spread_body(cells, own, got, mine, *rest):
    share = mine.shape[0]
    total = own[:, :cells] + got[:, :cells].astype(f32)
    part = resplit(own[:, cells:] + got[:, cells:].astype(f32))
    mine[:, :cells] = total[:share]
    mine[:, cells:] = part[:share]
    for k, out in enumerate(rest):
        rows = slice((k + 1) * share, (k + 2) * share)
        out[:, :cells] = total[rows].astype(bf16)
        out[:, cells:] = part[rows].astype(bf16)


def start_body(pairs, low, got_low, high, got_high, r, p):
    share, mid = r.shape[0] // pairs, low.shape[1]
    for b in range(pairs):
        rows = slice(b * share, (b + 1) * share)
        for v, got, k, columns in ((low, got_low, 3, slice(0, mid)), (high, got_high, 1, slice(mid, 2 * mid))):
            total = summed(v, got, k, b, share, slice(0, mid))
            r[rows, columns] = total
            p[rows, columns] = total.astype(bf16)


def update_body(pairs, low, got_low, high, got_high, old, q, r, p, sums):
    share, mid = r.shape[0] // pairs, low.shape[1]
    for b in range(pairs):
        rows = slice(b * share, (b + 1) * share)
        tail = summed(high, got_high, 1, b, share, slice(mid, None))
        tail = tail + pltpu.roll(tail, TAIL - 4, 1)
        if b == 0:
            sums[...] = tail
        alpha = tail[:, 0:1] / tail[:, 1:2]
        for v, got, k, columns in ((low, got_low, 3, slice(0, mid)), (high, got_high, 1, slice(mid, 2 * mid))):
            was = old[rows, columns]
            image = summed(v, got, k, b, share, slice(0, mid)) + damping * was
            new = was - alpha * image
            q[rows, columns] = image
            r[rows, columns] = new
            p[rows, columns] = new.astype(bf16)


def coeff_body(place, rank, bands, cross, pa, pb, *rest):
    if cross:
        qa, qb, l, out, norms, p = rest
    else:
        l, out, norms, p = rest
    half = pa.shape[0]
    p[:half, :] = pa[...]
    p[half:, :] = pb[...]
    width = l.shape[1]
    step = min(STEP, width)
    for j in range(0, width, step):
        put_blocks(out, dot(p[...], l[:, j:j + step]).astype(bf16).T, j // rank, place, rank)
    lane = lax.broadcasted_iota(jnp.int32, (half, TAIL), 1)
    for h, (now, old) in enumerate(((pa, qa), (pb, qb)) if cross else ((pa, None), (pb, None))):
        v = now[...].astype(f32)
        col = jnp.where(lane == 0, jnp.sum(v * v, axis=1, keepdims=True) * (1.0 / bands), 0.0)
        if cross:
            col = jnp.where(lane == 1, jnp.sum(v * old[...].astype(f32), axis=1, keepdims=True) * (1.0 / bands), col)
        norms[h * half:(h + 1) * half, :] = col


def middle_body(order, place, rank, cross, got, norms, r, *rest):
    if cross:
        old, out, seen, natural, turned = rest
    else:
        out, seen, natural, turned = rest
    take_blocks(got, natural, order, rank)
    width, cells = r.shape
    step = min(STEP, width)
    for j in range(0, width, step):
        turned[:, j:j + step] = natural[j:j + step, :].T
    step = min(STEP, cells)
    square = product = None
    for j in range(0, cells, step):
        s = dot(turned[...], r[:, j:j + step])
        seen[:, j:j + step] = s.astype(bf16)
        a = jnp.sum(s * s, axis=1, keepdims=True)
        square = a if square is None else square + a
        if cross:
            a = jnp.sum(s * old[:, j:j + step].astype(f32), axis=1, keepdims=True)
            product = a if product is None else product + a
    step = min(STEP, width)
    for j in range(0, width, step):
        back = dot(r[j:j + step, :], seen[...], ((1,), (1,))).astype(bf16)
        put_blocks(out, back, j // rank, place, rank)
    tile = norms[...]
    lane = lax.broadcasted_iota(jnp.int32, tile.shape, 1)
    pp, px = tile[:, 0:1], tile[:, 1:2]
    cols = jnp.where(lane == 0, pp, jnp.where(lane == 1, square + damping * pp, 0.0))
    if cross:
        cols = jnp.where(lane == 2, product + damping * px, cols)
    rows = cols.T[:8]
    low = rows - rows.astype(bf16).astype(f32)
    rows = jnp.concatenate([rows[0:1], low[0:1], rows[1:2], rows[2:3] if cross else low[1:2]], axis=0)
    half = rows.shape[1] // 2
    rows = jnp.concatenate([rows[:, :half], rows[:, half:]], axis=0).astype(bf16)
    for q in range(len(order)):
        out[q, 2 * rank:, :] = rows


def per_device(left_factor, right_factor, data):
    left, right, d = left_factor[0], right_factor[0], data[0]
    m, cells = d.shape
    width = left.shape[1]
    bands, blocks = lax.axis_size(BAND), lax.axis_size(SPACE)
    rank = width // blocks
    share, half, pairs = m // bands, m // 2, bands // 2
    order = order_of(blocks)
    place = [order.index(s) for s in range(blocks)]
    me = lax.axis_index(BAND)
    work = 2 * m * cells * width

    def exchange(v):
        return lax.all_to_all(v, SPACE, 0, 0, tiled=True, axis_index_groups=[order])

    def swap(v, flip):
        return lax.ppermute(v, BAND, [(i, i ^ flip) for i in range(bands)])

    def adjoint(got, scalars):
        columns = cells + (TAIL if scalars else 0)
        own, oth = call(
            functools.partial(adjoint_body, order, rank, scalars),
            [shape((half, columns), f32), shape((half, columns), bf16)],
            [pltpu.VMEM((width, m), bf16)], work, (got, left),
        )
        return own, swap(oth, 1)

    def along_y(own, got, tail):
        mid = cells // 2
        wide = mid + (TAIL if tail else 0)
        low, high = call(
            functools.partial(pair_body, cells, tail),
            [shape((half, mid), bf16), shape((half, wide), bf16)], [], own.size, (own, got),
        )
        got_low, got_high = swap(low, 2), swap(high, 6)

        def step(k, v, got):
            return call(functools.partial(step_body, k, pairs, mid), [shape(v.shape, bf16)], [], v.size, (v, got))[0]

        low, high = step(1, low, got_low), step(3, high, got_high)
        return low, swap(low, 6), high, swap(high, 2)

    def forward(now, old=()):
        coeff, norms = call(
            functools.partial(coeff_body, place, rank, bands, bool(old)),
            [shape((blocks, 2 * rank, half), bf16), shape((m, TAIL), f32)],
            [pltpu.VMEM((m, cells), bf16)], work, (*now, *old, left),
        )
        return exchange(coeff), norms

    def middle(got, norms, old=()):
        out, seen = call(
            functools.partial(middle_body, order, place, rank, bool(old)),
            [shape((blocks, 2 * rank + EXTRA, half), bf16), shape((m, cells), bf16)],
            [pltpu.VMEM((width, m), bf16), pltpu.VMEM((m, width), bf16)], 2 * work, (got, norms, right, *old),
        )
        return exchange(out), seen

    perm = jnp.stack([me ^ (2 * y + c) for c in range(2) for y in range(pairs)]).astype(jnp.int32)
    back = call(
        functools.partial(first_body, place, rank, share),
        [shape((blocks, 2 * rank, half), bf16)], [pltpu.VMEM((m, cells), bf16)], work, (perm, d, right),
        [SMEM, VMEM, VMEM],
    )[0]
    state = shape((half, cells), f32)
    parts = along_y(*adjoint(exchange(back), 0), False)
    r0, p0 = call(
        functools.partial(start_body, pairs), [state, shape((half, cells), bf16)], [], state.size, parts
    )
    p0 = (p0, swap(p0, 1))
    got, norms = forward(p0)
    got, s0 = middle(got, norms)
    parts = along_y(*adjoint(got, 2), True)
    q0, r1, p1, sums0 = call(
        functools.partial(update_body, pairs),
        [state, state, shape((half, cells), bf16), shape((share, TAIL), f32)], [], state.size, (*parts, r0),
    )
    p1 = (p1, swap(p1, 1))
    got, norms = forward(p1, p0)
    got, _ = middle(got, norms, (s0,))
    own, got = adjoint(got, 3)
    columns = cells + TAIL
    mine, *rest = call(
        functools.partial(spread_body, cells),
        [shape((share, columns), f32)] + [shape((share, columns), bf16)] * (pairs - 1),
        [], half * columns, (own, got),
    )
    total = mine
    for k in range(1, pairs):
        total = total + swap(rest[k - 1], 2 * k).astype(f32)
    sums1 = total[:, cells:cells + 4] + total[:, cells + 4:cells + 8]
    r0, q0, r1 = r0[:share], q0[:share], r1[:share]
    q1 = total[:, :cells] + damping * r1
    rr0, c0 = sums0[:, 0:1], sums0[:, 1:2]
    rr1, n11, n01 = sums1[:, 0:1], sums1[:, 1:2], sums1[:, 2:3]
    a0, b0 = rr0 / c0, rr1 / rr0
    a1 = rr1 / (n11 + 2 * b0 * n01 + b0 * b0 * c0)
    return a0 * r0 + a1 * (r1 + b0 * r0), r1 - a1 * (q1 + b0 * q0)


def solution(mesh):
    return jax.shard_map(
        per_device,
        mesh=mesh,
        in_specs=(P("band", "space", None), P("band", None, "space"), P("band", None, "space")),
        out_specs=(P("band", "space"), P("band", "space")),
        check_vma=False,
    )
```

```python
import functools
import jax
import jax.numpy as jnp
from jax import lax
from jax.experimental import pallas as pl
from jax.experimental.pallas import tpu as pltpu
from jax.sharding import PartitionSpec as P

damping = 1.0
BAND = "band"
SPACE = "space"
f32, bf16 = jnp.float32, jnp.bfloat16
EXTRA = 8
TAIL = 128
STEP = 256

VMEM = pl.BlockSpec(memory_space=pltpu.VMEM)
SMEM = pl.BlockSpec(memory_space=pltpu.SMEM)


def order_of(blocks):
    if blocks != 32:
        return list(range(blocks))
    return [(x if z % 2 == 0 else 3 - x) * 8 + z for z in range(8) for x in range(4)]


def dot(a, b, dims=((1,), (0,))):
    return lax.dot_general(a, b, (dims, ((), ())), preferred_element_type=f32)


def call(body, outs, scratch, flops, args, specs=None):
    moved = sum(a.size * a.dtype.itemsize for a in args) + sum(o.size * o.dtype.itemsize for o in outs)
    return pl.pallas_call(
        body,
        out_shape=outs,
        in_specs=specs or [VMEM] * len(args),
        out_specs=[VMEM] * len(outs),
        scratch_shapes=scratch,
        cost_estimate=pl.CostEstimate(flops=flops, bytes_accessed=moved, transcendentals=0),
        compiler_params=pltpu.CompilerParams(vmem_limit_bytes=40 * 1024 * 1024),
    )(*args)


def shape(dims, kind):
    return jax.ShapeDtypeStruct(dims, kind)


def put_blocks(out, rows, first, place, rank):
    half = rows.shape[1] // 2
    for i in range(rows.shape[0] // rank):
        block = rows[i * rank:(i + 1) * rank]
        out[place[first + i], :rank, :] = block[:, :half]
        out[place[first + i], rank:2 * rank, :] = block[:, half:]


def take_blocks(got, natural, order, rank):
    half = got.shape[2]
    for q, s in enumerate(order):
        natural[s * rank:(s + 1) * rank, :half] = got[q, :rank, :]
        natural[s * rank:(s + 1) * rank, half:] = got[q, rank:2 * rank, :]


def first_body(place, rank, share, perm, d, r, out, dp):
    for k in range(d.shape[0] // share):
        dp[k * share:(k + 1) * share, :] = d[pl.ds(pl.multiple_of(perm[k] * share, share), share), :]
    step = min(STEP, r.shape[0])
    for j in range(0, r.shape[0], step):
        put_blocks(out, dot(r[j:j + step, :], dp[...], ((1,), (1,))).astype(bf16), j // rank, place, rank)


def adjoint_body(order, rank, scalars, got, l, own, oth, natural):
    take_blocks(got, natural, order, rank)
    adjoint_rows(natural, l, 0, l.shape[0] // 2, own, oth)
    if scalars:
        rows = got[0, 2 * rank:, :].astype(f32)
        for q in range(1, len(order)):
            rows = rows + got[q, 2 * rank:, :].astype(f32)
        rows = jnp.concatenate([rows[:4], rows[4:]], axis=1)
        first = rows[0:1] + rows[1:2]
        zero = jnp.zeros_like(first)
        if scalars == 2:
            rows = [first, rows[2:3] + rows[3:4], zero, zero]
        else:
            rows = [first, rows[2:3], rows[3:4], zero]
        rows = jnp.concatenate(rows, axis=0)
        high = rows.astype(bf16).astype(f32)
        t = jnp.concatenate([high, rows - high, jnp.zeros((TAIL - 8, rows.shape[1]), f32)], axis=0).T
        mid, half = l.shape[0] // 2, own.shape[0]
        own[:, mid:] = t[:half]
        oth[:, mid:] = t[half:].astype(bf16)


def adjoint_rows(natural, l, begin, end, own, oth):
    half = own.shape[0]
    step = min(STEP, end - begin)
    for j in range(begin, end, step):
        t = dot(l[j:j + step, :], natural[...]).T
        columns = slice(j - begin, j - begin + step)
        own[:, columns] = t[:half]
        oth[:, columns] = t[half:].astype(bf16)


def adjoint_second_body(natural, l, own, oth):
    adjoint_rows(natural, l, l.shape[0] // 2, l.shape[0], own, oth)


def resplit(part):
    lane = lax.broadcasted_iota(jnp.int32, part.shape, 1)
    both = part + pltpu.roll(part, TAIL - 4, 1)
    high = both.astype(bf16).astype(f32)
    return jnp.where(lane < 4, high, jnp.where(lane < 8, pltpu.roll(both - high, 4, 1), 0.0))


def pair_body(mid, own, got, out):
    out[:, :mid] = (own[:, :mid] + got[:, :mid].astype(f32)).astype(bf16)
    if own.shape[1] > mid:
        out[:, mid:] = resplit(own[:, mid:] + got[:, mid:].astype(f32)).astype(bf16)


def summed(v, got, k, b, share, columns):
    rows, far = slice(b * share, (b + 1) * share), slice((b ^ k) * share, ((b ^ k) + 1) * share)
    return v[rows, columns].astype(f32) + got[far, columns].astype(f32)


def step_body(k, pairs, cells, v, got, out):
    share = v.shape[0] // pairs
    for b in range(pairs):
        rows = slice(b * share, (b + 1) * share)
        out[rows, :cells] = summed(v, got, k, b, share, slice(0, cells)).astype(bf16)
        if v.shape[1] > cells:
            out[rows, cells:] = resplit(summed(v, got, k, b, share, slice(cells, None))).astype(bf16)


def spread_body(low, got_low, high, got_high, mine, *rest):
    share, mid = mine.shape[0], high.shape[1]
    cells = 2 * mid
    total = low[:, :mid] + got_low[:, :mid].astype(f32)
    second = high[...] + got_high[...].astype(f32)
    part = resplit(low[:, mid:] + got_low[:, mid:].astype(f32))
    mine[:, :mid] = total[:share]
    mine[:, mid:cells] = second[:share]
    mine[:, cells:] = part[:share]
    for k, out in enumerate(rest):
        rows = slice((k + 1) * share, (k + 2) * share)
        out[:, :mid] = total[rows].astype(bf16)
        out[:, mid:cells] = second[rows].astype(bf16)
        out[:, cells:] = part[rows].astype(bf16)


def start_body(k, pairs, v, got, r, p):
    share = r.shape[0] // pairs
    for b in range(pairs):
        rows = slice(b * share, (b + 1) * share)
        total = summed(v, got, k, b, share, slice(None))
        r[rows, :] = total
        p[rows, :] = total.astype(bf16)


def update_body(k, pairs, first, v, got, old, *rest):
    if first:
        q, r, p, scalars = rest
    else:
        scalars, q, r, p = rest
    share, mid = r.shape[0] // pairs, r.shape[1]
    for b in range(pairs):
        rows = slice(b * share, (b + 1) * share)
        if first:
            tail = summed(v, got, k, b, share, slice(mid, None))
            scalars[rows, :] = tail + pltpu.roll(tail, TAIL - 4, 1)
        tail = scalars[rows, :]
        alpha = tail[:, 0:1] / tail[:, 1:2]
        was = old[rows, :]
        image = summed(v, got, k, b, share, slice(0, mid)) + damping * was
        new = was - alpha * image
        q[rows, :] = image
        r[rows, :] = new
        p[rows, :] = new.astype(bf16)


def coeff_body(place, rank, bands, cross, *refs):
    now, old, (l, out, norms, p) = refs[:4], refs[4:-4], refs[-4:]
    half, mid = now[0].shape
    lane = lax.broadcasted_iota(jnp.int32, (half, TAIL), 1)
    for h in range(2):
        rows = slice(h * half, (h + 1) * half)
        square = product = 0.0
        for c in range(2):
            v = now[2 * h + c][...]
            p[rows, c * mid:(c + 1) * mid] = v
            v = v.astype(f32)
            square = square + jnp.sum(v * v, axis=1, keepdims=True)
            if cross:
                product = product + jnp.sum(v * old[2 * h + c][...].astype(f32), axis=1, keepdims=True)
        col = jnp.where(lane == 0, square * (1.0 / bands), 0.0)
        if cross:
            col = jnp.where(lane == 1, product * (1.0 / bands), col)
        norms[rows, :] = col
    width = l.shape[1]
    step = min(STEP, width)
    for j in range(0, width, step):
        put_blocks(out, dot(p[...], l[:, j:j + step]).astype(bf16).T, j // rank, place, rank)


def middle_body(order, place, rank, cross, got, norms, r, *rest):
    if cross:
        old, out, seen, natural, turned = rest
    else:
        out, seen, natural, turned = rest
    take_blocks(got, natural, order, rank)
    width, cells = r.shape
    step = min(STEP, width)
    for j in range(0, width, step):
        turned[:, j:j + step] = natural[j:j + step, :].T
    step = min(STEP, cells)
    square = product = None
    for j in range(0, cells, step):
        s = dot(turned[...], r[:, j:j + step])
        seen[:, j:j + step] = s.astype(bf16)
        a = jnp.sum(s * s, axis=1, keepdims=True)
        square = a if square is None else square + a
        if cross:
            a = jnp.sum(s * old[:, j:j + step].astype(f32), axis=1, keepdims=True)
            product = a if product is None else product + a
    step = min(STEP, width)
    for j in range(0, width, step):
        back = dot(r[j:j + step, :], seen[...], ((1,), (1,))).astype(bf16)
        put_blocks(out, back, j // rank, place, rank)
    tile = norms[...]
    lane = lax.broadcasted_iota(jnp.int32, tile.shape, 1)
    pp, px = tile[:, 0:1], tile[:, 1:2]
    cols = jnp.where(lane == 0, pp, jnp.where(lane == 1, square + damping * pp, 0.0))
    if cross:
        cols = jnp.where(lane == 2, product + damping * px, cols)
    rows = cols.T[:8]
    low = rows - rows.astype(bf16).astype(f32)
    rows = jnp.concatenate([rows[0:1], low[0:1], rows[1:2], rows[2:3] if cross else low[1:2]], axis=0)
    half = rows.shape[1] // 2
    rows = jnp.concatenate([rows[:, :half], rows[:, half:]], axis=0).astype(bf16)
    for q in range(len(order)):
        out[q, 2 * rank:, :] = rows


def per_device(left_factor, right_factor, data):
    left, right, d = left_factor[0], right_factor[0], data[0]
    m, cells = d.shape
    width = left.shape[1]
    bands, blocks = lax.axis_size(BAND), lax.axis_size(SPACE)
    rank = width // blocks
    share, half, pairs = m // bands, m // 2, bands // 2
    mid = cells // 2
    order = order_of(blocks)
    place = [order.index(s) for s in range(blocks)]
    me = lax.axis_index(BAND)
    work = 2 * m * cells * width

    def exchange(v):
        return lax.all_to_all(v, SPACE, 0, 0, tiled=True, axis_index_groups=[order])

    def swap(v, flip):
        return lax.ppermute(v, BAND, [(i, i ^ flip) for i in range(bands)])

    def adjoint(got, scalars):
        wide = mid + (TAIL if scalars else 0)
        own, oth, natural = call(
            functools.partial(adjoint_body, order, rank, scalars),
            [shape((half, wide), f32), shape((half, wide), bf16), shape((width, m), bf16)], [], work // 2, (got, left),
        )
        low = own, swap(oth, 1)
        own, oth = call(
            adjoint_second_body, [shape((half, mid), f32), shape((half, mid), bf16)], [], work // 2, (natural, left)
        )
        return low, (own, swap(oth, 1))

    def along_y(k, own, got):
        v = call(functools.partial(pair_body, mid), [shape(got.shape, bf16)], [], own.size, (own, got))[0]
        got = swap(v, 2 * k)
        v = call(functools.partial(step_body, k, pairs, mid), [shape(v.shape, bf16)], [], v.size, (v, got))[0]
        return v, swap(v, 2 * (4 - k))

    def forward(now, old=()):
        coeff, norms = call(
            functools.partial(coeff_body, place, rank, bands, bool(old)),
            [shape((blocks, 2 * rank, half), bf16), shape((m, TAIL), f32)],
            [pltpu.VMEM((m, cells), bf16)], work, (*now, *old, left),
        )
        return exchange(coeff), norms

    def middle(got, norms, old=()):
        out, seen = call(
            functools.partial(middle_body, order, place, rank, bool(old)),
            [shape((blocks, 2 * rank + EXTRA, half), bf16), shape((m, cells), bf16)],
            [pltpu.VMEM((width, m), bf16), pltpu.VMEM((m, width), bf16)], 2 * work, (got, norms, right, *old),
        )
        return exchange(out), seen

    perm = jnp.stack([me ^ (2 * y + c) for c in range(2) for y in range(pairs)]).astype(jnp.int32)
    back = call(
        functools.partial(first_body, place, rank, share),
        [shape((blocks, 2 * rank, half), bf16)], [pltpu.VMEM((m, cells), bf16)], work, (perm, d, right),
        [SMEM, VMEM, VMEM],
    )[0]
    state, sent = shape((half, mid), f32), shape((half, mid), bf16)
    ways = (1, 3)
    r0, p0 = [], []
    for k, piece in zip(ways, adjoint(exchange(back), 0)):
        r, p = call(functools.partial(start_body, 4 - k, pairs), [state, sent], [], state.size, along_y(k, *piece))
        r0.append(r)
        p0.append(p)
    p0 += [swap(p, 1) for p in p0]
    got, norms = forward(p0)
    got, s0 = middle(got, norms)
    low, high = adjoint(got, 2)
    q, r, p, sums0 = call(
        functools.partial(update_body, 3, pairs, True),
        [state, state, sent, shape((half, TAIL), f32)], [], state.size, (*along_y(1, *low), r0[0]),
    )
    q0, r1, p1 = [q], [r], [p]
    q, r, p = call(
        functools.partial(update_body, 1, pairs, False),
        [state, state, sent], [], state.size, (*along_y(3, *high), r0[1], sums0),
    )
    q0, r1, p1 = q0 + [q], r1 + [r], p1 + [p]
    p1 += [swap(p, 1) for p in p1]
    got, norms = forward(p1, p0)
    got, _ = middle(got, norms, (s0,))
    low, high = adjoint(got, 3)
    columns = cells + TAIL
    mine, *rest = call(
        spread_body,
        [shape((share, columns), f32)] + [shape((share, columns), bf16)] * (pairs - 1),
        [], half * columns, (*low, *high),
    )
    total = mine
    for k in range(1, pairs):
        total = total + swap(rest[k - 1], 2 * k).astype(f32)
    sums1 = total[:, cells:cells + 4] + total[:, cells + 4:cells + 8]
    r0, q0, r1 = (jnp.concatenate([v[:share] for v in pair], axis=1) for pair in (r0, q0, r1))
    sums0 = sums0[:share]
    q1 = total[:, :cells] + damping * r1
    rr0, c0 = sums0[:, 0:1], sums0[:, 1:2]
    rr1, n11, n01 = sums1[:, 0:1], sums1[:, 1:2], sums1[:, 2:3]
    a0, b0 = rr0 / c0, rr1 / rr0
    a1 = rr1 / (n11 + 2 * b0 * n01 + b0 * b0 * c0)
    return a0 * r0 + a1 * (r1 + b0 * r0), r1 - a1 * (q1 + b0 * q0)


def solution(mesh):
    return jax.shard_map(
        per_device,
        mesh=mesh,
        in_specs=(P("band", "space", None), P("band", None, "space"), P("band", None, "space")),
        out_specs=(P("band", "space"), P("band", "space")),
        check_vma=False,
    )
```

```python
import functools
import jax
import jax.numpy as jnp
from jax import lax
from jax.experimental import pallas as pl
from jax.experimental.pallas import tpu as pltpu
from jax.sharding import PartitionSpec as P

damping = 1.0
BAND = "band"
SPACE = "space"
f32, bf16 = jnp.float32, jnp.bfloat16
EXTRA = 8
TAIL = 128
STEP = 256

VMEM = pl.BlockSpec(memory_space=pltpu.VMEM)
ANY = pl.BlockSpec(memory_space=pl.ANY)
SMEM = pl.BlockSpec(memory_space=pltpu.SMEM)


def order_of(blocks):
    if blocks != 32:
        return list(range(blocks))
    return [(x if z % 2 == 0 else 3 - x) * 8 + z for z in range(8) for x in range(4)]


def dot(a, b, dims=((1,), (0,))):
    return lax.dot_general(a, b, (dims, ((), ())), preferred_element_type=f32)


def call(body, outs, scratch, flops, args, specs=None):
    moved = sum(a.size * a.dtype.itemsize for a in args) + sum(o.size * o.dtype.itemsize for o in outs)
    return pl.pallas_call(
        body,
        out_shape=outs,
        in_specs=specs or [VMEM] * len(args),
        out_specs=[VMEM] * len(outs),
        scratch_shapes=scratch,
        cost_estimate=pl.CostEstimate(flops=flops, bytes_accessed=moved, transcendentals=0),
        compiler_params=pltpu.CompilerParams(vmem_limit_bytes=24 * 1024 * 1024),
    )(*args)


def shape(dims, kind):
    return jax.ShapeDtypeStruct(dims, kind)


def bring_body(a, out, sem):
    copy = pltpu.make_async_copy(a, out, sem)
    copy.start()
    copy.wait()


def put_blocks(out, rows, first, place, rank):
    half = rows.shape[1] // 2
    for i in range(rows.shape[0] // rank):
        block = rows[i * rank:(i + 1) * rank]
        out[place[first + i], :rank, :] = block[:, :half]
        out[place[first + i], rank:2 * rank, :] = block[:, half:]


def take_blocks(got, natural, order, rank):
    half = got.shape[2]
    for q, s in enumerate(order):
        natural[s * rank:(s + 1) * rank, :half] = got[q, :rank, :]
        natural[s * rank:(s + 1) * rank, half:] = got[q, rank:2 * rank, :]


def put_band(out, rows, first, place, rank, band):
    for i in range(rows.shape[0] // rank):
        out[place[first + i], band * rank:(band + 1) * rank, :] = rows[i * rank:(i + 1) * rank]


def take_band(got, natural, order, rank, band):
    width = len(order) * rank
    for q, s in enumerate(order):
        natural[band * width + s * rank:band * width + (s + 1) * rank, :] = got[q, band * rank:(band + 1) * rank, :]


def first_body(place, rank, share, perm, d, r, out, dp):
    for k in range(d.shape[0] // share):
        dp[k * share:(k + 1) * share, :] = d[pl.ds(pl.multiple_of(perm[k] * share, share), share), :]
    step = min(STEP, r.shape[0])
    for j in range(0, r.shape[0], step):
        put_blocks(out, dot(r[j:j + step, :], dp[...], ((1,), (1,))).astype(bf16), j // rank, place, rank)


def adjoint_body(order, rank, got, l, own, oth, natural):
    take_blocks(got, natural, order, rank)
    adjoint_rows(natural, l, 0, l.shape[0] // 2, own, oth)


def adjoint_rows(natural, l, begin, end, own, oth):
    half = own.shape[0]
    step = min(STEP, end - begin)
    for j in range(begin, end, step):
        t = dot(l[j:j + step, :], natural[...]).T
        columns = slice(j - begin, j - begin + step)
        own[:, columns] = t[:half]
        oth[:, columns] = t[half:].astype(bf16)


def adjoint_second_body(natural, l, own, oth):
    adjoint_rows(natural, l, l.shape[0] // 2, l.shape[0], own, oth)


def both_rows(natural, l, other, begin, end, out):
    width = l.shape[1]
    step = min(STEP, end - begin)
    for j in range(begin, end, step):
        t = dot(l[j:j + step, :], natural[:width, :]) + dot(other[j:j + step, :], natural[width:, :])
        out[:, j - begin:j - begin + step] = t.T.astype(out.dtype)


def both_body(order, rank, got, l, other, out, natural):
    for band in range(2):
        take_band(got, natural, order, rank, band)
    mid = l.shape[0] // 2
    both_rows(natural, l, other, 0, mid, out)
    rows = got[0, 2 * rank:, :].astype(f32)
    for q in range(1, len(order)):
        rows = rows + got[q, 2 * rank:, :].astype(f32)
    rows = rows[:4] + rows[4:]
    high = rows.astype(bf16).astype(f32)
    t = jnp.concatenate([high, rows - high, jnp.zeros((TAIL - 8, rows.shape[1]), f32)], axis=0).T
    out[:, mid:] = t.astype(out.dtype)


def both_second_body(natural, l, other, out):
    both_rows(natural, l, other, l.shape[0] // 2, l.shape[0], out)


def resplit(part):
    lane = lax.broadcasted_iota(jnp.int32, part.shape, 1)
    both = part + pltpu.roll(part, TAIL - 4, 1)
    high = both.astype(bf16).astype(f32)
    return jnp.where(lane < 4, high, jnp.where(lane < 8, pltpu.roll(both - high, 4, 1), 0.0))


def pair_body(mid, own, got, out):
    out[:, :mid] = (own[:, :mid] + got[:, :mid].astype(f32)).astype(bf16)
    if own.shape[1] > mid:
        out[:, mid:] = resplit(own[:, mid:] + got[:, mid:].astype(f32)).astype(bf16)


def summed(v, got, k, b, share, columns):
    rows, far = slice(b * share, (b + 1) * share), slice((b ^ k) * share, ((b ^ k) + 1) * share)
    return v[rows, columns].astype(f32) + got[far, columns].astype(f32)


def step_body(k, pairs, cells, v, got, out):
    share = v.shape[0] // pairs
    for b in range(pairs):
        rows = slice(b * share, (b + 1) * share)
        out[rows, :cells] = summed(v, got, k, b, share, slice(0, cells)).astype(bf16)
        if v.shape[1] > cells:
            out[rows, cells:] = resplit(summed(v, got, k, b, share, slice(cells, None))).astype(bf16)


def spread_body(low, high, mine, *rest):
    share, mid = mine.shape[0], high.shape[1]
    cells = 2 * mid
    for k, out in enumerate((mine, *rest)):
        rows = slice(k * share, (k + 1) * share)
        out[:, :mid] = low[rows, :mid].astype(out.dtype)
        out[:, mid:cells] = high[rows, :].astype(out.dtype)
        out[:, cells:] = low[rows, mid:].astype(out.dtype)


def start_body(k, pairs, v, got, r, p):
    share = r.shape[0] // pairs
    for b in range(pairs):
        rows = slice(b * share, (b + 1) * share)
        total = summed(v, got, k, b, share, slice(None))
        r[rows, :] = total
        p[rows, :] = total.astype(bf16)


def update_body(k, pairs, first, v, got, old, *rest):
    if first:
        q, r, p, scalars = rest
    else:
        scalars, q, r, p = rest
    share, mid = r.shape[0] // pairs, r.shape[1]
    for b in range(pairs):
        rows = slice(b * share, (b + 1) * share)
        if first:
            tail = summed(v, got, k, b, share, slice(mid, None))
            scalars[rows, :] = tail + pltpu.roll(tail, TAIL - 4, 1)
        tail = scalars[rows, :]
        alpha = tail[:, 0:1] / tail[:, 1:2]
        was = old[rows, :]
        image = summed(v, got, k, b, share, slice(0, mid)) + damping * was
        new = was - alpha * image
        q[rows, :] = image
        r[rows, :] = new
        p[rows, :] = new.astype(bf16)


def coeff_body(place, rank, copies, cross, *refs):
    now, old, (l, other, out, norms, p) = refs[:2], refs[2:-5], refs[-5:]
    half, mid = now[0].shape
    lane = lax.broadcasted_iota(jnp.int32, (half, TAIL), 1)
    square = product = 0.0
    for c in range(2):
        v = now[c][...]
        p[:, c * mid:(c + 1) * mid] = v
        v = v.astype(f32)
        square = square + jnp.sum(v * v, axis=1, keepdims=True)
        if cross:
            product = product + jnp.sum(v * old[c][...].astype(f32), axis=1, keepdims=True)
    col = jnp.where(lane == 0, square * (1.0 / copies), 0.0)
    if cross:
        col = jnp.where(lane == 1, product * (1.0 / copies), col)
    norms[...] = col
    width = l.shape[1]
    step = min(STEP, width)
    for band, factor in enumerate((l, other)):
        for j in range(0, width, step):
            put_band(out, dot(p[...], factor[:, j:j + step]).astype(bf16).T, j // rank, place, rank, band)


def middle_body(order, place, rank, cross, got, norms, r, other, *rest):
    if cross:
        old, out, seen, natural, turned = rest
    else:
        out, seen, natural, turned = rest
    width, cells = r.shape
    half = got.shape[2]
    square = product = 0.0
    for band, factor in enumerate((r, other)):
        take_band(got, natural, order, rank, band)
        images = slice(band * half, (band + 1) * half)
        step = min(STEP, width)
        for j in range(0, width, step):
            turned[images, j:j + step] = natural[band * width + j:band * width + j + step, :].T
        step = min(STEP, cells)
        for j in range(0, cells, step):
            s = dot(turned[images, :], factor[:, j:j + step])
            seen[images, j:j + step] = s.astype(bf16)
            square = square + jnp.sum(s * s, axis=1, keepdims=True)
            if cross:
                product = product + jnp.sum(s * old[images, j:j + step].astype(f32), axis=1, keepdims=True)
        step = min(STEP, width)
        for j in range(0, width, step):
            back = dot(factor[j:j + step, :], seen[images, :], ((1,), (1,))).astype(bf16)
            put_band(out, back, j // rank, place, rank, band)
    tile = norms[...]
    lane = lax.broadcasted_iota(jnp.int32, tile.shape, 1)
    pp, px = tile[:, 0:1], tile[:, 1:2]
    cols = jnp.where(lane == 0, pp, jnp.where(lane == 1, square + damping * pp, 0.0))
    if cross:
        cols = jnp.where(lane == 2, product + damping * px, cols)
    rows = cols.T[:4]
    high = rows.astype(bf16).astype(f32)
    rows = jnp.concatenate([high, rows - high], axis=0).astype(bf16)
    for q in range(len(order)):
        out[q, 2 * rank:, :] = rows


def per_device(left_factor, right_factor, data):
    left, right, d = left_factor[0], right_factor[0], data[0]
    m, cells = d.shape
    width = left.shape[1]
    bands, blocks = lax.axis_size(BAND), lax.axis_size(SPACE)
    rank = width // blocks
    share, half, pairs = m // bands, m // 2, bands // 2
    mid = cells // 2
    order = order_of(blocks)
    place = [order.index(s) for s in range(blocks)]
    me = lax.axis_index(BAND)
    work = 2 * m * cells * width

    def exchange(v):
        return lax.all_to_all(v, SPACE, 0, 0, tiled=True, axis_index_groups=[order])

    def swap(v, flip):
        return lax.ppermute(v, BAND, [(i, i ^ flip) for i in range(bands)])

    left_other, right_other = swap(left, 1), swap(right, 1)

    def adjoint(got):
        own, oth, natural = call(
            functools.partial(adjoint_body, order, rank),
            [shape((half, mid), f32), shape((half, mid), bf16), shape((width, m), bf16)], [], work // 2, (got, left),
        )
        low = own, swap(oth, 1)
        own, oth = call(
            adjoint_second_body, [shape((half, mid), f32), shape((half, mid), bf16)], [], work // 2, (natural, left)
        )
        return [
            call(functools.partial(pair_body, mid), [shape((half, mid), bf16)], [], half * mid, piece)[0]
            for piece in (low, (own, swap(oth, 1)))
        ]

    def adjoint_both(got, kind):
        low, natural = call(
            functools.partial(both_body, order, rank),
            [shape((half, mid + TAIL), kind), shape((2 * width, half), bf16)], [], work // 2, (got, left, left_other),
        )
        high = call(both_second_body, [shape((half, mid), kind)], [], work // 2, (natural, left, left_other))[0]
        return low, high

    def along_y(k, v):
        got = swap(v, 2 * k)
        v = call(functools.partial(step_body, k, pairs, mid), [shape(v.shape, bf16)], [], v.size, (v, got))[0]
        return v, swap(v, 2 * (4 - k))

    def forward(now, old=()):
        coeff, norms = call(
            functools.partial(coeff_body, place, rank, pairs, bool(old)),
            [shape((blocks, 2 * rank, half), bf16), shape((half, TAIL), f32)],
            [pltpu.VMEM((half, cells), bf16)], work, (*now, *old, left, left_other),
        )
        return exchange(coeff), norms

    def middle(got, norms, old=()):
        out, seen = call(
            functools.partial(middle_body, order, place, rank, bool(old)),
            [shape((blocks, 2 * rank + EXTRA, half), bf16), shape((m, cells), bf16)],
            [pltpu.VMEM((2 * width, half), bf16), pltpu.VMEM((m, width), bf16)], 2 * work,
            (got, norms, right, right_other, *old),
        )
        return exchange(out), seen

    perm = jnp.stack([me ^ (2 * y + c) for c in range(2) for y in range(pairs)]).astype(jnp.int32)
    back = call(
        functools.partial(first_body, place, rank, share),
        [shape((blocks, 2 * rank, half), bf16)], [pltpu.VMEM((m, cells), bf16)], work, (perm, d, right),
        [SMEM, VMEM, VMEM],
    )[0]
    state, sent = shape((half, mid), f32), shape((half, mid), bf16)
    ways = (1, 3)
    r0, p0 = [], []
    got, left_other, right_other = lax.optimization_barrier((exchange(back), left_other, right_other))
    left_other, right_other = (
        call(bring_body, [shape(v.shape, bf16)], [pltpu.SemaphoreType.DMA], 0, (v,), [ANY])[0]
        for v in (left_other, right_other)
    )
    for k, piece in zip(ways, adjoint(got)):
        r, p = call(functools.partial(start_body, 4 - k, pairs), [state, sent], [], state.size, along_y(k, piece))
        r0.append(r)
        p0.append(p)
    p0, left_other, right_other = lax.optimization_barrier((p0, left_other, right_other))
    got, norms = forward(p0)
    got, s0 = middle(got, norms)
    low, high = adjoint_both(got, bf16)
    q, r, p, sums0 = call(
        functools.partial(update_body, 3, pairs, True),
        [state, state, sent, shape((half, TAIL), f32)], [], state.size, (*along_y(1, low), r0[0]),
    )
    q0, r1, p1 = [q], [r], [p]
    q, r, p = call(
        functools.partial(update_body, 1, pairs, False),
        [state, state, sent], [], state.size, (*along_y(3, high), r0[1], sums0),
    )
    q0, r1, p1 = q0 + [q], r1 + [r], p1 + [p]
    got, norms = forward(p1, p0)
    got, _ = middle(got, norms, (s0,))
    low, high = adjoint_both(got, f32)
    columns = cells + TAIL
    mine, *rest = call(
        spread_body,
        [shape((share, columns), f32)] + [shape((share, columns), bf16)] * (pairs - 1),
        [], half * columns, (low, high),
    )
    total = mine
    for k in range(1, pairs):
        total = total + swap(rest[k - 1], 2 * k).astype(f32)
    sums1 = total[:, cells:cells + 4] + total[:, cells + 4:cells + 8]
    r0, q0, r1 = (jnp.concatenate([v[:share] for v in pair], axis=1) for pair in (r0, q0, r1))
    sums0 = sums0[:share]
    q1 = total[:, :cells] + damping * r1
    rr0, c0 = sums0[:, 0:1], sums0[:, 1:2]
    rr1, n11, n01 = sums1[:, 0:1], sums1[:, 1:2], sums1[:, 2:3]
    a0, b0 = rr0 / c0, rr1 / rr0
    a1 = rr1 / (n11 + 2 * b0 * n01 + b0 * b0 * c0)
    return a0 * r0 + a1 * (r1 + b0 * r0), r1 - a1 * (q1 + b0 * q0)


def solution(mesh):
    return jax.shard_map(
        per_device,
        mesh=mesh,
        in_specs=(P("band", "space", None), P("band", None, "space"), P("band", None, "space")),
        out_specs=(P("band", "space"), P("band", "space")),
        check_vma=False,
    )
```

```python
import functools
import jax
import jax.numpy as jnp
from jax import lax
from jax.experimental import pallas as pl
from jax.experimental.pallas import tpu as pltpu
from jax.sharding import PartitionSpec as P

damping = 1.0
BAND = "band"
SPACE = "space"
f32, bf16 = jnp.float32, jnp.bfloat16
EXTRA = 8
TAIL = 128
STEP = 256

VMEM = pl.BlockSpec(memory_space=pltpu.VMEM)
ANY = pl.BlockSpec(memory_space=pl.ANY)
SMEM = pl.BlockSpec(memory_space=pltpu.SMEM)


def order_of(blocks):
    if blocks != 32:
        return list(range(blocks))
    return [x * 8 + z for z in range(8) for x in range(4)]


def dot(a, b, dims=((1,), (0,))):
    return lax.dot_general(a, b, (dims, ((), ())), preferred_element_type=f32)


def call(body, outs, scratch, flops, args, specs=None):
    moved = sum(a.size * a.dtype.itemsize for a in args) + sum(o.size * o.dtype.itemsize for o in outs)
    return pl.pallas_call(
        body,
        out_shape=outs,
        in_specs=specs or [VMEM] * len(args),
        out_specs=[VMEM] * len(outs),
        scratch_shapes=scratch,
        cost_estimate=pl.CostEstimate(flops=flops, bytes_accessed=moved, transcendentals=0),
        compiler_params=pltpu.CompilerParams(vmem_limit_bytes=24 * 1024 * 1024),
    )(*args)


def shape(dims, kind):
    return jax.ShapeDtypeStruct(dims, kind)


def bring_body(a, out, sem):
    copy = pltpu.make_async_copy(a, out, sem)
    copy.start()
    copy.wait()


def put_blocks(out, rows, first, place, rank):
    half = rows.shape[1] // 2
    for i in range(rows.shape[0] // rank):
        block = rows[i * rank:(i + 1) * rank]
        out[place[first + i], :rank, :] = block[:, :half]
        out[place[first + i], rank:2 * rank, :] = block[:, half:]


def take_blocks(got, natural, order, rank):
    half = got.shape[2]
    for q, s in enumerate(order):
        natural[s * rank:(s + 1) * rank, :half] = got[q, :rank, :]
        natural[s * rank:(s + 1) * rank, half:] = got[q, rank:2 * rank, :]


def put_band(out, rows, first, place, rank, band):
    for i in range(rows.shape[0] // rank):
        out[place[first + i], band * rank:(band + 1) * rank, :] = rows[i * rank:(i + 1) * rank]


def take_band(got, natural, order, rank, band):
    width = len(order) * rank
    for q, s in enumerate(order):
        natural[band * width + s * rank:band * width + (s + 1) * rank, :] = got[q, band * rank:(band + 1) * rank, :]


def first_body(place, rank, share, perm, d, r, out, dp):
    for k in range(d.shape[0] // share):
        dp[k * share:(k + 1) * share, :] = d[pl.ds(pl.multiple_of(perm[k] * share, share), share), :]
    step = min(STEP, r.shape[0])
    for j in range(0, r.shape[0], step):
        put_blocks(out, dot(r[j:j + step, :], dp[...], ((1,), (1,))).astype(bf16), j // rank, place, rank)


def adjoint_body(order, rank, got, l, own, oth, natural):
    take_blocks(got, natural, order, rank)
    adjoint_rows(natural, l, 0, l.shape[0] // 2, own, oth)


def adjoint_rows(natural, l, begin, end, own, oth):
    half = own.shape[0]
    step = min(STEP, end - begin)
    for j in range(begin, end, step):
        t = dot(l[j:j + step, :], natural[...]).T
        columns = slice(j - begin, j - begin + step)
        own[:, columns] = t[:half]
        oth[:, columns] = t[half:].astype(bf16)


def adjoint_second_body(natural, l, own, oth):
    adjoint_rows(natural, l, l.shape[0] // 2, l.shape[0], own, oth)


def both_rows(natural, l, other, begin, end, out):
    width = l.shape[1]
    step = min(STEP, end - begin)
    for j in range(begin, end, step):
        t = dot(l[j:j + step, :], natural[:width, :]) + dot(other[j:j + step, :], natural[width:, :])
        out[:, j - begin:j - begin + step] = t.T.astype(out.dtype)


def both_body(order, rank, got, l, other, out, natural):
    for band in range(2):
        take_band(got, natural, order, rank, band)
    mid = l.shape[0] // 2
    both_rows(natural, l, other, 0, mid, out)
    rows = got[0, 2 * rank:, :].astype(f32)
    for q in range(1, len(order)):
        rows = rows + got[q, 2 * rank:, :].astype(f32)
    rows = rows[:4] + rows[4:]
    high = rows.astype(bf16).astype(f32)
    t = jnp.concatenate([high, rows - high, jnp.zeros((TAIL - 8, rows.shape[1]), f32)], axis=0).T
    out[:, mid:] = t.astype(out.dtype)


def both_second_body(natural, l, other, out):
    both_rows(natural, l, other, l.shape[0] // 2, l.shape[0], out)


def resplit(part):
    lane = lax.broadcasted_iota(jnp.int32, part.shape, 1)
    both = part + pltpu.roll(part, TAIL - 4, 1)
    high = both.astype(bf16).astype(f32)
    return jnp.where(lane < 4, high, jnp.where(lane < 8, pltpu.roll(both - high, 4, 1), 0.0))


def pair_body(mid, own, got, out):
    out[:, :mid] = (own[:, :mid] + got[:, :mid].astype(f32)).astype(bf16)
    if own.shape[1] > mid:
        out[:, mid:] = resplit(own[:, mid:] + got[:, mid:].astype(f32)).astype(bf16)


def summed(v, got, k, b, share, columns):
    rows, far = slice(b * share, (b + 1) * share), slice((b ^ k) * share, ((b ^ k) + 1) * share)
    return v[rows, columns].astype(f32) + got[far, columns].astype(f32)


def step_body(k, pairs, cells, v, got, out):
    share = v.shape[0] // pairs
    for b in range(pairs):
        rows = slice(b * share, (b + 1) * share)
        out[rows, :cells] = summed(v, got, k, b, share, slice(0, cells)).astype(bf16)
        if v.shape[1] > cells:
            out[rows, cells:] = resplit(summed(v, got, k, b, share, slice(cells, None))).astype(bf16)


def spread_body(low, high, mine, *rest):
    share, mid = mine.shape[0], high.shape[1]
    cells = 2 * mid
    for k, out in enumerate((mine, *rest)):
        rows = slice(k * share, (k + 1) * share)
        out[:, :mid] = low[rows, :mid].astype(out.dtype)
        out[:, mid:cells] = high[rows, :].astype(out.dtype)
        out[:, cells:] = low[rows, mid:].astype(out.dtype)


def start_body(k, pairs, v, got, r, p):
    share = r.shape[0] // pairs
    for b in range(pairs):
        rows = slice(b * share, (b + 1) * share)
        total = summed(v, got, k, b, share, slice(None))
        r[rows, :] = total
        p[rows, :] = total.astype(bf16)


def update_body(k, pairs, first, v, got, old, *rest):
    if first:
        q, r, p, scalars = rest
    else:
        scalars, q, r, p = rest
    share, mid = r.shape[0] // pairs, r.shape[1]
    for b in range(pairs):
        rows = slice(b * share, (b + 1) * share)
        if first:
            tail = summed(v, got, k, b, share, slice(mid, None))
            scalars[rows, :] = tail + pltpu.roll(tail, TAIL - 4, 1)
        tail = scalars[rows, :]
        alpha = tail[:, 0:1] / tail[:, 1:2]
        was = old[rows, :]
        image = summed(v, got, k, b, share, slice(0, mid)) + damping * was
        new = was - alpha * image
        q[rows, :] = image
        r[rows, :] = new
        p[rows, :] = new.astype(bf16)


def coeff_body(place, rank, copies, cross, *refs):
    now, old, (l, other, out, norms, p) = refs[:2], refs[2:-5], refs[-5:]
    half, mid = now[0].shape
    lane = lax.broadcasted_iota(jnp.int32, (half, TAIL), 1)
    square = product = 0.0
    for c in range(2):
        v = now[c][...]
        p[:, c * mid:(c + 1) * mid] = v
        v = v.astype(f32)
        square = square + jnp.sum(v * v, axis=1, keepdims=True)
        if cross:
            product = product + jnp.sum(v * old[c][...].astype(f32), axis=1, keepdims=True)
    col = jnp.where(lane == 0, square * (1.0 / copies), 0.0)
    if cross:
        col = jnp.where(lane == 1, product * (1.0 / copies), col)
    norms[...] = col
    width = l.shape[1]
    step = min(STEP, width)
    for band, factor in enumerate((l, other)):
        for j in range(0, width, step):
            put_band(out, dot(p[...], factor[:, j:j + step]).astype(bf16).T, j // rank, place, rank, band)


def middle_body(order, place, rank, cross, got, norms, r, other, *rest):
    fetch = None
    if cross:
        old, out, seen, natural, turned = rest
    else:
        out, seen, kept, natural, turned, sem = rest
        fetch = pltpu.make_async_copy(other, kept, sem)
        fetch.start()
        other = kept
    width, cells = r.shape
    half = got.shape[2]
    square = product = 0.0
    for band, factor in enumerate((r, other)):
        take_band(got, natural, order, rank, band)
        if band and fetch is not None:
            fetch.wait()
        images = slice(band * half, (band + 1) * half)
        step = min(STEP, width)
        for j in range(0, width, step):
            turned[images, j:j + step] = natural[band * width + j:band * width + j + step, :].T
        step = min(STEP, cells)
        for j in range(0, cells, step):
            s = dot(turned[images, :], factor[:, j:j + step])
            seen[images, j:j + step] = s.astype(bf16)
            square = square + jnp.sum(s * s, axis=1, keepdims=True)
            if cross:
                product = product + jnp.sum(s * old[images, j:j + step].astype(f32), axis=1, keepdims=True)
        step = min(STEP, width)
        for j in range(0, width, step):
            back = dot(factor[j:j + step, :], seen[images, :], ((1,), (1,))).astype(bf16)
            put_band(out, back, j // rank, place, rank, band)
    tile = norms[...]
    lane = lax.broadcasted_iota(jnp.int32, tile.shape, 1)
    pp, px = tile[:, 0:1], tile[:, 1:2]
    cols = jnp.where(lane == 0, pp, jnp.where(lane == 1, square + damping * pp, 0.0))
    if cross:
        cols = jnp.where(lane == 2, product + damping * px, cols)
    rows = cols.T[:4]
    high = rows.astype(bf16).astype(f32)
    rows = jnp.concatenate([high, rows - high], axis=0).astype(bf16)
    for q in range(len(order)):
        out[q, 2 * rank:, :] = rows


def per_device(left_factor, right_factor, data):
    left, right, d = left_factor[0], right_factor[0], data[0]
    m, cells = d.shape
    width = left.shape[1]
    bands, blocks = lax.axis_size(BAND), lax.axis_size(SPACE)
    rank = width // blocks
    share, half, pairs = m // bands, m // 2, bands // 2
    mid = cells // 2
    order = order_of(blocks)
    place = [order.index(s) for s in range(blocks)]
    me = lax.axis_index(BAND)
    work = 2 * m * cells * width

    def exchange(v):
        return lax.all_to_all(v, SPACE, 0, 0, tiled=True, axis_index_groups=[order])

    def swap(v, flip):
        return lax.ppermute(v, BAND, [(i, i ^ flip) for i in range(bands)])

    left_other, right_other = swap(left, 1), swap(right, 1)

    def adjoint(got):
        own, oth, natural = call(
            functools.partial(adjoint_body, order, rank),
            [shape((half, mid), f32), shape((half, mid), bf16), shape((width, m), bf16)], [], work // 2, (got, left),
        )
        low = own, swap(oth, 1)
        own, oth = call(
            adjoint_second_body, [shape((half, mid), f32), shape((half, mid), bf16)], [], work // 2, (natural, left)
        )
        return [
            call(functools.partial(pair_body, mid), [shape((half, mid), bf16)], [], half * mid, piece)[0]
            for piece in (low, (own, swap(oth, 1)))
        ]

    def adjoint_both(got, kind):
        low, natural = call(
            functools.partial(both_body, order, rank),
            [shape((half, mid + TAIL), kind), shape((2 * width, half), bf16)], [], work // 2, (got, left, left_other),
        )
        high = call(both_second_body, [shape((half, mid), kind)], [], work // 2, (natural, left, left_other))[0]
        return low, high

    def along_y(k, v):
        got = swap(v, 2 * k)
        v = call(functools.partial(step_body, k, pairs, mid), [shape(v.shape, bf16)], [], v.size, (v, got))[0]
        return v, swap(v, 2 * (4 - k))

    def forward(now, old=()):
        coeff, norms = call(
            functools.partial(coeff_body, place, rank, pairs, bool(old)),
            [shape((blocks, 2 * rank, half), bf16), shape((half, TAIL), f32)],
            [pltpu.VMEM((half, cells), bf16)], work, (*now, *old, left, left_other),
        )
        return exchange(coeff), norms

    def middle(got, norms, other, old=()):
        outs = [shape((blocks, 2 * rank + EXTRA, half), bf16), shape((m, cells), bf16)]
        scratch = [pltpu.VMEM((2 * width, half), bf16), pltpu.VMEM((m, width), bf16)]
        specs = [VMEM] * (4 + len(old))
        if not old:
            outs.append(shape(other.shape, bf16))
            scratch.append(pltpu.SemaphoreType.DMA)
            specs[3] = ANY
        out, seen, *kept = call(
            functools.partial(middle_body, order, place, rank, bool(old)),
            outs, scratch, 2 * work, (got, norms, right, other, *old), specs,
        )
        return exchange(out), seen, kept

    perm = jnp.stack([me ^ (2 * y + c) for c in range(2) for y in range(pairs)]).astype(jnp.int32)
    back = call(
        functools.partial(first_body, place, rank, share),
        [shape((blocks, 2 * rank, half), bf16)], [pltpu.VMEM((m, cells), bf16)], work, (perm, d, right),
        [SMEM, VMEM, VMEM],
    )[0]
    state, sent = shape((half, mid), f32), shape((half, mid), bf16)
    ways = (1, 3)
    r0, p0 = [], []
    got, left_other, right_other = lax.optimization_barrier((exchange(back), left_other, right_other))
    left_other = call(
        bring_body, [shape(left.shape, bf16)], [pltpu.SemaphoreType.DMA], 0, (left_other,), [ANY]
    )[0]
    for k, piece in zip(ways, adjoint(got)):
        r, p = call(functools.partial(start_body, 4 - k, pairs), [state, sent], [], state.size, along_y(k, piece))
        r0.append(r)
        p0.append(p)
    p0, left_other = lax.optimization_barrier((p0, left_other))
    got, norms = forward(p0)
    got, s0, (right_other,) = middle(got, norms, right_other)
    low, high = adjoint_both(got, bf16)
    q, r, p, sums0 = call(
        functools.partial(update_body, 3, pairs, True),
        [state, state, sent, shape((half, TAIL), f32)], [], state.size, (*along_y(1, low), r0[0]),
    )
    q0, r1, p1 = [q], [r], [p]
    q, r, p = call(
        functools.partial(update_body, 1, pairs, False),
        [state, state, sent], [], state.size, (*along_y(3, high), r0[1], sums0),
    )
    q0, r1, p1 = q0 + [q], r1 + [r], p1 + [p]
    got, norms = forward(p1, p0)
    got, _, _ = middle(got, norms, right_other, (s0,))
    low, high = adjoint_both(got, f32)
    columns = cells + TAIL
    mine, *rest = call(
        spread_body,
        [shape((share, columns), f32)] + [shape((share, columns), bf16)] * (pairs - 1),
        [], half * columns, (low, high),
    )
    total = mine
    for k in range(1, pairs):
        total = total + swap(rest[k - 1], 2 * k).astype(f32)
    sums1 = total[:, cells:cells + 4] + total[:, cells + 4:cells + 8]
    r0, q0, r1 = (jnp.concatenate([v[:share] for v in pair], axis=1) for pair in (r0, q0, r1))
    sums0 = sums0[:share]
    q1 = total[:, :cells] + damping * r1
    rr0, c0 = sums0[:, 0:1], sums0[:, 1:2]
    rr1, n11, n01 = sums1[:, 0:1], sums1[:, 1:2], sums1[:, 2:3]
    a0, b0 = rr0 / c0, rr1 / rr0
    a1 = rr1 / (n11 + 2 * b0 * n01 + b0 * b0 * c0)
    return a0 * r0 + a1 * (r1 + b0 * r0), r1 - a1 * (q1 + b0 * q0)


def solution(mesh):
    return jax.shard_map(
        per_device,
        mesh=mesh,
        in_specs=(P("band", "space", None), P("band", None, "space"), P("band", None, "space")),
        out_specs=(P("band", "space"), P("band", "space")),
        check_vma=False,
    )
```

```python
import functools
import jax
import jax.numpy as jnp
from jax import lax
from jax.experimental import pallas as pl
from jax.experimental.pallas import tpu as pltpu
from jax.sharding import PartitionSpec as P

damping = 1.0
BAND = "band"
SPACE = "space"
f32, bf16 = jnp.float32, jnp.bfloat16
EXTRA = 8
TAIL = 128
STEP = 512

VMEM = pl.BlockSpec(memory_space=pltpu.VMEM)
ANY = pl.BlockSpec(memory_space=pl.ANY)
SMEM = pl.BlockSpec(memory_space=pltpu.SMEM)


def order_of(blocks):
    if blocks != 32:
        return list(range(blocks))
    return [x * 8 + (z + x) % 8 for z in range(8) for x in range(4)]


def dot(a, b, dims=((1,), (0,))):
    return lax.dot_general(a, b, (dims, ((), ())), preferred_element_type=f32)


def call(body, outs, scratch, flops, args, specs=None):
    moved = sum(a.size * a.dtype.itemsize for a in args) + sum(o.size * o.dtype.itemsize for o in outs)
    return pl.pallas_call(
        body,
        out_shape=outs,
        in_specs=specs or [VMEM] * len(args),
        out_specs=[VMEM] * len(outs),
        scratch_shapes=scratch,
        cost_estimate=pl.CostEstimate(flops=flops, bytes_accessed=moved, transcendentals=0),
        compiler_params=pltpu.CompilerParams(vmem_limit_bytes=24 * 1024 * 1024),
    )(*args)


def shape(dims, kind):
    return jax.ShapeDtypeStruct(dims, kind)


def bring_body(a, out, sem):
    copy = pltpu.make_async_copy(a, out, sem)
    copy.start()
    copy.wait()


def put_blocks(out, rows, first, place, rank):
    half = rows.shape[1] // 2
    for i in range(rows.shape[0] // rank):
        block = rows[i * rank:(i + 1) * rank]
        out[place[first + i], :rank, :] = block[:, :half]
        out[place[first + i], rank:2 * rank, :] = block[:, half:]


def take_blocks(got, natural, order, rank):
    half = got.shape[2]
    for q, s in enumerate(order):
        natural[s * rank:(s + 1) * rank, :half] = got[q, :rank, :]
        natural[s * rank:(s + 1) * rank, half:] = got[q, rank:2 * rank, :]


def put_band(out, rows, first, place, rank, band):
    for i in range(rows.shape[0] // rank):
        out[place[first + i], band * rank:(band + 1) * rank, :] = rows[i * rank:(i + 1) * rank]


def take_band(got, natural, order, rank, band):
    width = len(order) * rank
    for q, s in enumerate(order):
        natural[band * width + s * rank:band * width + (s + 1) * rank, :] = got[q, band * rank:(band + 1) * rank, :]


def first_body(place, rank, share, perm, d, r, out, dp):
    for k in range(d.shape[0] // share):
        dp[k * share:(k + 1) * share, :] = d[pl.ds(pl.multiple_of(perm[k] * share, share), share), :]
    step = min(STEP, r.shape[0])
    for j in range(0, r.shape[0], step):
        put_blocks(out, dot(r[j:j + step, :], dp[...], ((1,), (1,))).astype(bf16), j // rank, place, rank)


def adjoint_body(order, rank, got, l, own, oth, natural):
    take_blocks(got, natural, order, rank)
    adjoint_rows(natural, l, 0, l.shape[0] // 2, own, oth)


def adjoint_rows(natural, l, begin, end, own, oth):
    half = own.shape[0]
    step = min(STEP, end - begin)
    for j in range(begin, end, step):
        t = dot(l[j:j + step, :], natural[...]).T
        columns = slice(j - begin, j - begin + step)
        own[:, columns] = t[:half]
        oth[:, columns] = t[half:].astype(bf16)


def adjoint_second_body(natural, l, own, oth):
    adjoint_rows(natural, l, l.shape[0] // 2, l.shape[0], own, oth)


def both_rows(natural, l, other, begin, end, out):
    width = l.shape[1]
    step = min(STEP, end - begin)
    for j in range(begin, end, step):
        t = dot(l[j:j + step, :], natural[:width, :]) + dot(other[j:j + step, :], natural[width:, :])
        out[:, j - begin:j - begin + step] = t.T.astype(out.dtype)


def both_body(order, rank, got, l, other, out, natural):
    for band in range(2):
        take_band(got, natural, order, rank, band)
    mid = l.shape[0] // 2
    both_rows(natural, l, other, 0, mid, out)
    rows = got[0, 2 * rank:, :].astype(f32)
    for q in range(1, len(order)):
        rows = rows + got[q, 2 * rank:, :].astype(f32)
    rows = rows[:4] + rows[4:]
    high = rows.astype(bf16).astype(f32)
    t = jnp.concatenate([high, rows - high, jnp.zeros((TAIL - 8, rows.shape[1]), f32)], axis=0).T
    out[:, mid:] = t.astype(out.dtype)


def both_second_body(natural, l, other, out):
    both_rows(natural, l, other, l.shape[0] // 2, l.shape[0], out)


def resplit(part):
    lane = lax.broadcasted_iota(jnp.int32, part.shape, 1)
    both = part + pltpu.roll(part, TAIL - 4, 1)
    high = both.astype(bf16).astype(f32)
    return jnp.where(lane < 4, high, jnp.where(lane < 8, pltpu.roll(both - high, 4, 1), 0.0))


def pair_body(mid, own, got, out):
    out[:, :mid] = (own[:, :mid] + got[:, :mid].astype(f32)).astype(bf16)
    if own.shape[1] > mid:
        out[:, mid:] = resplit(own[:, mid:] + got[:, mid:].astype(f32)).astype(bf16)


def summed(v, got, k, b, share, columns):
    rows, far = slice(b * share, (b + 1) * share), slice((b ^ k) * share, ((b ^ k) + 1) * share)
    return v[rows, columns].astype(f32) + got[far, columns].astype(f32)


def step_body(k, pairs, cells, v, got, out):
    share = v.shape[0] // pairs
    for b in range(pairs):
        rows = slice(b * share, (b + 1) * share)
        out[rows, :cells] = summed(v, got, k, b, share, slice(0, cells)).astype(bf16)
        if v.shape[1] > cells:
            out[rows, cells:] = resplit(summed(v, got, k, b, share, slice(cells, None))).astype(bf16)


def spread_body(low, high, mine, *rest):
    share, mid = mine.shape[0], high.shape[1]
    cells = 2 * mid
    for k, out in enumerate((mine, *rest)):
        rows = slice(k * share, (k + 1) * share)
        out[:, :mid] = low[rows, :mid].astype(out.dtype)
        out[:, mid:cells] = high[rows, :].astype(out.dtype)
        out[:, cells:] = low[rows, mid:].astype(out.dtype)


def start_body(k, pairs, v, got, r, p):
    share = r.shape[0] // pairs
    for b in range(pairs):
        rows = slice(b * share, (b + 1) * share)
        total = summed(v, got, k, b, share, slice(None))
        r[rows, :] = total
        p[rows, :] = total.astype(bf16)


def update_body(k, pairs, first, v, got, old, *rest):
    if first:
        q, r, p, scalars = rest
    else:
        scalars, q, r, p = rest
    share, mid = r.shape[0] // pairs, r.shape[1]
    for b in range(pairs):
        rows = slice(b * share, (b + 1) * share)
        if first:
            tail = summed(v, got, k, b, share, slice(mid, None))
            scalars[rows, :] = tail + pltpu.roll(tail, TAIL - 4, 1)
        tail = scalars[rows, :]
        alpha = tail[:, 0:1] / tail[:, 1:2]
        was = old[rows, :]
        image = summed(v, got, k, b, share, slice(0, mid)) + damping * was
        new = was - alpha * image
        q[rows, :] = image
        r[rows, :] = new
        p[rows, :] = new.astype(bf16)


def coeff_body(place, rank, copies, cross, *refs):
    now, old, (l, other, out, norms, p) = refs[:2], refs[2:-5], refs[-5:]
    half, mid = now[0].shape
    lane = lax.broadcasted_iota(jnp.int32, (half, TAIL), 1)
    square = product = 0.0
    for c in range(2):
        v = now[c][...]
        p[:, c * mid:(c + 1) * mid] = v
        v = v.astype(f32)
        square = square + jnp.sum(v * v, axis=1, keepdims=True)
        if cross:
            product = product + jnp.sum(v * old[c][...].astype(f32), axis=1, keepdims=True)
    col = jnp.where(lane == 0, square * (1.0 / copies), 0.0)
    if cross:
        col = jnp.where(lane == 1, product * (1.0 / copies), col)
    norms[...] = col
    width = l.shape[1]
    step = min(STEP, width)
    for band, factor in enumerate((l, other)):
        for j in range(0, width, step):
            put_band(out, dot(p[...], factor[:, j:j + step]).astype(bf16).T, j // rank, place, rank, band)


def middle_body(order, place, rank, cross, got, norms, r, other, *rest):
    fetch = None
    if cross:
        old, out, seen, natural, turned = rest
    else:
        out, seen, kept, natural, turned, sem = rest
        fetch = pltpu.make_async_copy(other, kept, sem)
        fetch.start()
        other = kept
    width, cells = r.shape
    half = got.shape[2]
    square = product = 0.0
    for band, factor in enumerate((r, other)):
        take_band(got, natural, order, rank, band)
        if band and fetch is not None:
            fetch.wait()
        images = slice(band * half, (band + 1) * half)
        step = min(STEP, width)
        for j in range(0, width, step):
            turned[images, j:j + step] = natural[band * width + j:band * width + j + step, :].T
        step = min(STEP, cells)
        for j in range(0, cells, step):
            s = dot(turned[images, :], factor[:, j:j + step])
            seen[images, j:j + step] = s.astype(bf16)
            square = square + jnp.sum(s * s, axis=1, keepdims=True)
            if cross:
                product = product + jnp.sum(s * old[images, j:j + step].astype(f32), axis=1, keepdims=True)
        step = min(STEP, width)
        for j in range(0, width, step):
            back = dot(factor[j:j + step, :], seen[images, :], ((1,), (1,))).astype(bf16)
            put_band(out, back, j // rank, place, rank, band)
    tile = norms[...]
    lane = lax.broadcasted_iota(jnp.int32, tile.shape, 1)
    pp, px = tile[:, 0:1], tile[:, 1:2]
    cols = jnp.where(lane == 0, pp, jnp.where(lane == 1, square + damping * pp, 0.0))
    if cross:
        cols = jnp.where(lane == 2, product + damping * px, cols)
    rows = cols.T[:4]
    high = rows.astype(bf16).astype(f32)
    rows = jnp.concatenate([high, rows - high], axis=0).astype(bf16)
    for q in range(len(order)):
        out[q, 2 * rank:, :] = rows


def per_device(left_factor, right_factor, data):
    left, right, d = left_factor[0], right_factor[0], data[0]
    m, cells = d.shape
    width = left.shape[1]
    bands, blocks = lax.axis_size(BAND), lax.axis_size(SPACE)
    rank = width // blocks
    share, half, pairs = m // bands, m // 2, bands // 2
    mid = cells // 2
    order = order_of(blocks)
    place = [order.index(s) for s in range(blocks)]
    me = lax.axis_index(BAND)
    work = 2 * m * cells * width

    def exchange(v):
        return lax.all_to_all(v, SPACE, 0, 0, tiled=True, axis_index_groups=[order])

    def swap(v, flip):
        return lax.ppermute(v, BAND, [(i, i ^ flip) for i in range(bands)])

    left_other, right_other = swap(left, 1), swap(right, 1)

    def adjoint(got):
        own, oth, natural = call(
            functools.partial(adjoint_body, order, rank),
            [shape((half, mid), f32), shape((half, mid), bf16), shape((width, m), bf16)], [], work // 2, (got, left),
        )
        low = own, swap(oth, 1)
        own, oth = call(
            adjoint_second_body, [shape((half, mid), f32), shape((half, mid), bf16)], [], work // 2, (natural, left)
        )
        return [
            call(functools.partial(pair_body, mid), [shape((half, mid), bf16)], [], half * mid, piece)[0]
            for piece in (low, (own, swap(oth, 1)))
        ]

    def adjoint_both(got, kind):
        low, natural = call(
            functools.partial(both_body, order, rank),
            [shape((half, mid + TAIL), kind), shape((2 * width, half), bf16)], [], work // 2, (got, left, left_other),
        )
        high = call(both_second_body, [shape((half, mid), kind)], [], work // 2, (natural, left, left_other))[0]
        return low, high

    def along_y(k, v):
        got = swap(v, 2 * k)
        v = call(functools.partial(step_body, k, pairs, mid), [shape(v.shape, bf16)], [], v.size, (v, got))[0]
        return v, swap(v, 2 * (4 - k))

    def forward(now, old=()):
        coeff, norms = call(
            functools.partial(coeff_body, place, rank, pairs, bool(old)),
            [shape((blocks, 2 * rank, half), bf16), shape((half, TAIL), f32)],
            [pltpu.VMEM((half, cells), bf16)], work, (*now, *old, left, left_other),
        )
        return exchange(coeff), norms

    def middle(got, norms, other, old=()):
        outs = [shape((blocks, 2 * rank + EXTRA, half), bf16), shape((m, cells), bf16)]
        scratch = [pltpu.VMEM((2 * width, half), bf16), pltpu.VMEM((m, width), bf16)]
        specs = [VMEM] * (4 + len(old))
        if not old:
            outs.append(shape(other.shape, bf16))
            scratch.append(pltpu.SemaphoreType.DMA)
            specs[3] = ANY
        out, seen, *kept = call(
            functools.partial(middle_body, order, place, rank, bool(old)),
            outs, scratch, 2 * work, (got, norms, right, other, *old), specs,
        )
        return exchange(out), seen, kept

    perm = jnp.stack([me ^ (2 * y + c) for c in range(2) for y in range(pairs)]).astype(jnp.int32)
    back = call(
        functools.partial(first_body, place, rank, share),
        [shape((blocks, 2 * rank, half), bf16)], [pltpu.VMEM((m, cells), bf16)], work, (perm, d, right),
        [SMEM, VMEM, VMEM],
    )[0]
    state, sent = shape((half, mid), f32), shape((half, mid), bf16)
    ways = (1, 3)
    r0, p0 = [], []
    got, left_other, right_other = lax.optimization_barrier((exchange(back), left_other, right_other))
    left_other = call(
        bring_body, [shape(left.shape, bf16)], [pltpu.SemaphoreType.DMA], 0, (left_other,), [ANY]
    )[0]
    for k, piece in zip(ways, adjoint(got)):
        r, p = call(functools.partial(start_body, 4 - k, pairs), [state, sent], [], state.size, along_y(k, piece))
        r0.append(r)
        p0.append(p)
    p0, left_other = lax.optimization_barrier((p0, left_other))
    got, norms = forward(p0)
    got, s0, (right_other,) = middle(got, norms, right_other)
    low, high = adjoint_both(got, bf16)
    q, r, p, sums0 = call(
        functools.partial(update_body, 3, pairs, True),
        [state, state, sent, shape((half, TAIL), f32)], [], state.size, (*along_y(1, low), r0[0]),
    )
    q0, r1, p1 = [q], [r], [p]
    q, r, p = call(
        functools.partial(update_body, 1, pairs, False),
        [state, state, sent], [], state.size, (*along_y(3, high), r0[1], sums0),
    )
    q0, r1, p1 = q0 + [q], r1 + [r], p1 + [p]
    got, norms = forward(p1, p0)
    got, _, _ = middle(got, norms, right_other, (s0,))
    low, high = adjoint_both(got, f32)
    columns = cells + TAIL
    mine, *rest = call(
        spread_body,
        [shape((share, columns), f32)] + [shape((share, columns), bf16)] * (pairs - 1),
        [], half * columns, (low, high),
    )
    total = mine
    for k in range(1, pairs):
        total = total + swap(rest[k - 1], 2 * k).astype(f32)
    sums1 = total[:, cells:cells + 4] + total[:, cells + 4:cells + 8]
    r0, q0, r1 = (jnp.concatenate([v[:share] for v in pair], axis=1) for pair in (r0, q0, r1))
    sums0 = sums0[:share]
    q1 = total[:, :cells] + damping * r1
    rr0, c0 = sums0[:, 0:1], sums0[:, 1:2]
    rr1, n11, n01 = sums1[:, 0:1], sums1[:, 1:2], sums1[:, 2:3]
    a0, b0 = rr0 / c0, rr1 / rr0
    a1 = rr1 / (n11 + 2 * b0 * n01 + b0 * b0 * c0)
    return a0 * r0 + a1 * (r1 + b0 * r0), r1 - a1 * (q1 + b0 * q0)


def solution(mesh):
    return jax.shard_map(
        per_device,
        mesh=mesh,
        in_specs=(P("band", "space", None), P("band", None, "space"), P("band", None, "space")),
        out_specs=(P("band", "space"), P("band", "space")),
        check_vma=False,
    )
```

```python
import functools
import jax
import jax.numpy as jnp
from jax import lax
from jax.experimental import pallas as pl
from jax.experimental.pallas import tpu as pltpu
from jax.sharding import PartitionSpec as P

damping = 1.0
BAND = "band"
SPACE = "space"
f32, bf16 = jnp.float32, jnp.bfloat16
EXTRA = 8
TAIL = 128
STEP = 512

VMEM = pl.BlockSpec(memory_space=pltpu.VMEM)
ANY = pl.BlockSpec(memory_space=pl.ANY)
SMEM = pl.BlockSpec(memory_space=pltpu.SMEM)


def order_of(blocks):
    if blocks != 32:
        return list(range(blocks))
    return [x * 8 + (z + x) % 8 for z in range(8) for x in range(4)]


def dot(a, b, dims=((1,), (0,))):
    return lax.dot_general(a, b, (dims, ((), ())), preferred_element_type=f32)


def call(body, outs, scratch, flops, args, specs=None):
    moved = sum(a.size * a.dtype.itemsize for a in args) + sum(o.size * o.dtype.itemsize for o in outs)
    return pl.pallas_call(
        body,
        out_shape=outs,
        in_specs=specs or [VMEM] * len(args),
        out_specs=[VMEM] * len(outs),
        scratch_shapes=scratch,
        cost_estimate=pl.CostEstimate(flops=flops, bytes_accessed=moved, transcendentals=0),
        compiler_params=pltpu.CompilerParams(vmem_limit_bytes=24 * 1024 * 1024),
    )(*args)


def shape(dims, kind):
    return jax.ShapeDtypeStruct(dims, kind)


def bring_body(a, out, sem):
    copy = pltpu.make_async_copy(a, out, sem)
    copy.start()
    copy.wait()


def put_blocks(out, rows, first, place, rank):
    half = rows.shape[1] // 2
    for i in range(rows.shape[0] // rank):
        block = rows[i * rank:(i + 1) * rank]
        out[place[first + i], :rank, :] = block[:, :half]
        out[place[first + i], rank:2 * rank, :] = block[:, half:]


def take_blocks(got, natural, order, rank):
    half = got.shape[2]
    for q, s in enumerate(order):
        natural[s * rank:(s + 1) * rank, :half] = got[q, :rank, :]
        natural[s * rank:(s + 1) * rank, half:] = got[q, rank:2 * rank, :]


def put_band(out, rows, first, place, rank, band):
    for i in range(rows.shape[0] // rank):
        out[place[first + i], band * rank:(band + 1) * rank, :] = rows[i * rank:(i + 1) * rank]


def take_band(got, natural, order, rank, band):
    width = len(order) * rank
    for q, s in enumerate(order):
        natural[band * width + s * rank:band * width + (s + 1) * rank, :] = got[q, band * rank:(band + 1) * rank, :]


def first_body(place, rank, share, perm, d, r, out, dp):
    for k in range(d.shape[0] // share):
        dp[k * share:(k + 1) * share, :] = d[pl.ds(pl.multiple_of(perm[k] * share, share), share), :]
    step = min(STEP, r.shape[0])
    for j in range(0, r.shape[0], step):
        put_blocks(out, dot(r[j:j + step, :], dp[...], ((1,), (1,))).astype(bf16), j // rank, place, rank)


def adjoint_body(order, rank, got, l, own, oth, natural):
    take_blocks(got, natural, order, rank)
    adjoint_rows(natural, l, 0, l.shape[0] // 2, own, oth)


def adjoint_rows(natural, l, begin, end, own, oth):
    half = own.shape[0]
    step = min(STEP, end - begin)
    for j in range(begin, end, step):
        t = dot(l[j:j + step, :], natural[...]).T
        columns = slice(j - begin, j - begin + step)
        own[:, columns] = t[:half]
        oth[:, columns] = t[half:].astype(bf16)


def adjoint_second_body(natural, l, own, oth):
    adjoint_rows(natural, l, l.shape[0] // 2, l.shape[0], own, oth)


def both_rows(natural, l, other, begin, end, out):
    width = l.shape[1]
    step = min(STEP, end - begin)
    for j in range(begin, end, step):
        t = dot(l[j:j + step, :], natural[:width, :]) + dot(other[j:j + step, :], natural[width:, :])
        out[:, j - begin:j - begin + step] = t.T.astype(out.dtype)


def both_body(order, rank, got, l, other, out, natural):
    for band in range(2):
        take_band(got, natural, order, rank, band)
    mid = l.shape[0] // 2
    both_rows(natural, l, other, 0, mid, out)
    rows = got[0, 2 * rank:, :].astype(f32)
    for q in range(1, len(order)):
        rows = rows + got[q, 2 * rank:, :].astype(f32)
    rows = rows[:4] + rows[4:]
    high = rows.astype(bf16).astype(f32)
    t = jnp.concatenate([high, rows - high, jnp.zeros((TAIL - 8, rows.shape[1]), f32)], axis=0).T
    out[:, mid:] = t.astype(out.dtype)


def both_second_body(natural, l, other, out):
    both_rows(natural, l, other, l.shape[0] // 2, l.shape[0], out)


def resplit(part):
    lane = lax.broadcasted_iota(jnp.int32, part.shape, 1)
    both = part + pltpu.roll(part, TAIL - 4, 1)
    high = both.astype(bf16).astype(f32)
    return jnp.where(lane < 4, high, jnp.where(lane < 8, pltpu.roll(both - high, 4, 1), 0.0))


def pair_body(mid, own, got, out):
    out[:, :mid] = (own[:, :mid] + got[:, :mid].astype(f32)).astype(bf16)
    if own.shape[1] > mid:
        out[:, mid:] = resplit(own[:, mid:] + got[:, mid:].astype(f32)).astype(bf16)


def summed(v, got, k, b, share, columns):
    rows, far = slice(b * share, (b + 1) * share), slice((b ^ k) * share, ((b ^ k) + 1) * share)
    return v[rows, columns].astype(f32) + got[far, columns].astype(f32)


def step_body(k, pairs, cells, v, got, out):
    share = v.shape[0] // pairs
    for b in range(pairs):
        rows = slice(b * share, (b + 1) * share)
        out[rows, :cells] = summed(v, got, k, b, share, slice(0, cells)).astype(bf16)
        if v.shape[1] > cells:
            out[rows, cells:] = resplit(summed(v, got, k, b, share, slice(cells, None))).astype(bf16)


def spread_body(low, high, mine, *rest):
    share, mid = mine.shape[0], high.shape[1]
    cells = 2 * mid
    for k, out in enumerate((mine, *rest)):
        rows = slice(k * share, (k + 1) * share)
        out[:, :mid] = low[rows, :mid].astype(out.dtype)
        out[:, mid:cells] = high[rows, :].astype(out.dtype)
        out[:, cells:] = low[rows, mid:].astype(out.dtype)


def start_body(k, pairs, v, got, r, p):
    share = r.shape[0] // pairs
    for b in range(pairs):
        rows = slice(b * share, (b + 1) * share)
        total = summed(v, got, k, b, share, slice(None))
        r[rows, :] = total
        p[rows, :] = total.astype(bf16)


def update_body(k, pairs, first, v, got, old, *rest):
    if first:
        q, r, p, scalars = rest
    else:
        scalars, q, r, p = rest
    share, mid = r.shape[0] // pairs, r.shape[1]
    for b in range(pairs):
        rows = slice(b * share, (b + 1) * share)
        if first:
            tail = summed(v, got, k, b, share, slice(mid, None))
            scalars[rows, :] = tail + pltpu.roll(tail, TAIL - 4, 1)
        tail = scalars[rows, :]
        alpha = tail[:, 0:1] / tail[:, 1:2]
        was = old[rows, :]
        image = summed(v, got, k, b, share, slice(0, mid)) + damping * was
        new = was - alpha * image
        q[rows, :] = image
        r[rows, :] = new
        p[rows, :] = new.astype(bf16)


def coeff_body(place, rank, copies, cross, *refs):
    now, old, (l, other, out, norms, p) = refs[:2], refs[2:-5], refs[-5:]
    half, mid = now[0].shape
    lane = lax.broadcasted_iota(jnp.int32, (half, TAIL), 1)
    square = product = 0.0
    for c in range(2):
        v = now[c][...]
        p[:, c * mid:(c + 1) * mid] = v
        v = v.astype(f32)
        square = square + jnp.sum(v * v, axis=1, keepdims=True)
        if cross:
            product = product + jnp.sum(v * old[c][...].astype(f32), axis=1, keepdims=True)
    col = jnp.where(lane == 0, square * (1.0 / copies), 0.0)
    if cross:
        col = jnp.where(lane == 1, product * (1.0 / copies), col)
    norms[...] = col
    width = l.shape[1]
    step = min(STEP, width)
    for band, factor in enumerate((l, other)):
        for j in range(0, width, step):
            put_band(out, dot(p[...], factor[:, j:j + step]).astype(bf16).T, j // rank, place, rank, band)


def middle_body(order, place, rank, cross, got, norms, r, other, *rest):
    fetch = None
    if cross:
        old, out, seen, natural, turned = rest
    else:
        out, seen, kept, natural, turned, sem = rest
        fetch = pltpu.make_async_copy(other, kept, sem)
        fetch.start()
        other = kept
    width, cells = r.shape
    half = got.shape[2]
    square = product = 0.0
    for band, factor in enumerate((r, other)):
        take_band(got, natural, order, rank, band)
        if band and fetch is not None:
            fetch.wait()
        images = slice(band * half, (band + 1) * half)
        step = min(STEP, width)
        for j in range(0, width, step):
            turned[images, j:j + step] = natural[band * width + j:band * width + j + step, :].T
        step = min(STEP, cells)
        for j in range(0, cells, step):
            s = dot(turned[images, :], factor[:, j:j + step])
            seen[images, j:j + step] = s.astype(bf16)
            square = square + jnp.sum(s * s, axis=1, keepdims=True)
            if cross:
                product = product + jnp.sum(s * old[images, j:j + step].astype(f32), axis=1, keepdims=True)
        step = min(STEP, width)
        for j in range(0, width, step):
            back = dot(factor[j:j + step, :], seen[images, :], ((1,), (1,))).astype(bf16)
            put_band(out, back, j // rank, place, rank, band)
    tile = norms[...]
    lane = lax.broadcasted_iota(jnp.int32, tile.shape, 1)
    pp, px = tile[:, 0:1], tile[:, 1:2]
    cols = jnp.where(lane == 0, pp, jnp.where(lane == 1, square + damping * pp, 0.0))
    if cross:
        cols = jnp.where(lane == 2, product + damping * px, cols)
    rows = cols.T[:4]
    high = rows.astype(bf16).astype(f32)
    rows = jnp.concatenate([high, rows - high], axis=0).astype(bf16)
    for q in range(len(order)):
        out[q, 2 * rank:, :] = rows


def per_device(left_factor, right_factor, data):
    left, right, d = left_factor[0], right_factor[0], data[0]
    m, cells = d.shape
    width = left.shape[1]
    bands, blocks = lax.axis_size(BAND), lax.axis_size(SPACE)
    rank = width // blocks
    share, half, pairs = m // bands, m // 2, bands // 2
    mid = cells // 2
    order = order_of(blocks)
    place = [order.index(s) for s in range(blocks)]
    me = lax.axis_index(BAND)
    work = 2 * m * cells * width

    def exchange(v):
        return lax.all_to_all(v, SPACE, 0, 0, tiled=True, axis_index_groups=[order])

    def swap(v, flip):
        return lax.ppermute(v, BAND, [(i, i ^ flip) for i in range(bands)])

    def adjoint(got):
        own, oth, natural = call(
            functools.partial(adjoint_body, order, rank),
            [shape((half, mid), f32), shape((half, mid), bf16), shape((width, m), bf16)], [], work // 2, (got, left),
        )
        low = own, swap(oth, 1)
        own, oth = call(
            adjoint_second_body, [shape((half, mid), f32), shape((half, mid), bf16)], [], work // 2, (natural, left)
        )
        return [
            call(functools.partial(pair_body, mid), [shape((half, mid), bf16)], [], half * mid, piece)[0]
            for piece in (low, (own, swap(oth, 1)))
        ]

    def adjoint_both(got, kind):
        low, natural = call(
            functools.partial(both_body, order, rank),
            [shape((half, mid + TAIL), kind), shape((2 * width, half), bf16)], [], work // 2, (got, left, left_other),
        )
        high = call(both_second_body, [shape((half, mid), kind)], [], work // 2, (natural, left, left_other))[0]
        return low, high

    def along_y(k, v):
        got = swap(v, 2 * k)
        v = call(functools.partial(step_body, k, pairs, mid), [shape(v.shape, bf16)], [], v.size, (v, got))[0]
        return v, swap(v, 2 * (4 - k))

    def forward(now, old=()):
        coeff, norms = call(
            functools.partial(coeff_body, place, rank, pairs, bool(old)),
            [shape((blocks, 2 * rank, half), bf16), shape((half, TAIL), f32)],
            [pltpu.VMEM((half, cells), bf16)], work, (*now, *old, left, left_other),
        )
        return exchange(coeff), norms

    def middle(got, norms, other, old=()):
        outs = [shape((blocks, 2 * rank + EXTRA, half), bf16), shape((m, cells), bf16)]
        scratch = [pltpu.VMEM((2 * width, half), bf16), pltpu.VMEM((m, width), bf16)]
        specs = [VMEM] * (4 + len(old))
        if not old:
            outs.append(shape(other.shape, bf16))
            scratch.append(pltpu.SemaphoreType.DMA)
            specs[3] = ANY
        out, seen, *kept = call(
            functools.partial(middle_body, order, place, rank, bool(old)),
            outs, scratch, 2 * work, (got, norms, right, other, *old), specs,
        )
        return exchange(out), seen, kept

    perm = jnp.stack([me ^ (2 * y + c) for c in range(2) for y in range(pairs)]).astype(jnp.int32)
    back = call(
        functools.partial(first_body, place, rank, share),
        [shape((blocks, 2 * rank, half), bf16)], [pltpu.VMEM((m, cells), bf16)], work, (perm, d, right),
        [SMEM, VMEM, VMEM],
    )[0]
    back, mine = lax.optimization_barrier((back, (left, right)))
    left_other, right_other = swap(mine[0], 1), swap(mine[1], 1)
    state, sent = shape((half, mid), f32), shape((half, mid), bf16)
    ways = (1, 3)
    r0, p0 = [], []
    got, left_other, right_other = lax.optimization_barrier((exchange(back), left_other, right_other))
    left_other = call(
        bring_body, [shape(left.shape, bf16)], [pltpu.SemaphoreType.DMA], 0, (left_other,), [ANY]
    )[0]
    for k, piece in zip(ways, adjoint(got)):
        r, p = call(functools.partial(start_body, 4 - k, pairs), [state, sent], [], state.size, along_y(k, piece))
        r0.append(r)
        p0.append(p)
    p0, left_other = lax.optimization_barrier((p0, left_other))
    got, norms = forward(p0)
    got, s0, (right_other,) = middle(got, norms, right_other)
    low, high = adjoint_both(got, bf16)
    q, r, p, sums0 = call(
        functools.partial(update_body, 3, pairs, True),
        [state, state, sent, shape((half, TAIL), f32)], [], state.size, (*along_y(1, low), r0[0]),
    )
    q0, r1, p1 = [q], [r], [p]
    q, r, p = call(
        functools.partial(update_body, 1, pairs, False),
        [state, state, sent], [], state.size, (*along_y(3, high), r0[1], sums0),
    )
    q0, r1, p1 = q0 + [q], r1 + [r], p1 + [p]
    got, norms = forward(p1, p0)
    got, _, _ = middle(got, norms, right_other, (s0,))
    low, high = adjoint_both(got, f32)
    columns = cells + TAIL
    mine, *rest = call(
        spread_body,
        [shape((share, columns), f32)] + [shape((share, columns), bf16)] * (pairs - 1),
        [], half * columns, (low, high),
    )
    total = mine
    for k in range(1, pairs):
        total = total + swap(rest[k - 1], 2 * k).astype(f32)
    sums1 = total[:, cells:cells + 4] + total[:, cells + 4:cells + 8]
    r0, q0, r1 = (jnp.concatenate([v[:share] for v in pair], axis=1) for pair in (r0, q0, r1))
    sums0 = sums0[:share]
    q1 = total[:, :cells] + damping * r1
    rr0, c0 = sums0[:, 0:1], sums0[:, 1:2]
    rr1, n11, n01 = sums1[:, 0:1], sums1[:, 1:2], sums1[:, 2:3]
    a0, b0 = rr0 / c0, rr1 / rr0
    a1 = rr1 / (n11 + 2 * b0 * n01 + b0 * b0 * c0)
    return a0 * r0 + a1 * (r1 + b0 * r0), r1 - a1 * (q1 + b0 * q0)


def solution(mesh):
    return jax.shard_map(
        per_device,
        mesh=mesh,
        in_specs=(P("band", "space", None), P("band", None, "space"), P("band", None, "space")),
        out_specs=(P("band", "space"), P("band", "space")),
        check_vma=False,
    )
```
